32 devices in a mesh: dp: 8 (over y, x, core), tensor: 4 (over z).
Axes of the slice: x: 2, y: 2, z: 4, core: 2. Of those that a mesh axis runs over, the one named last changes fastest.
Arguments:
- inputs: bfloat16 [12288, 1024], P(('dp', 'tensor')), may hold values from -6 to 6
- cotangent: bfloat16 [12288, 1024], P(('dp', 'tensor')), may hold values from -6 to 6
- attn_gain: bfloat16 [1024], P(('dp', 'tensor')), may hold values from 0.5 to 1.5
- moe_gain: bfloat16 [1024], P(('dp', 'tensor')), may hold values from 0.5 to 1.5
- router: bfloat16 [1024, 4], P(('dp', 'tensor')), may hold values from -0.125 to 0.125
- w_query: bfloat16 [1024, 1024], P('dp', 'tensor'), may hold values from -0.1875 to 0.1875
- w_key: bfloat16 [1024, 1024], P('dp', 'tensor'), may hold values from -0.1875 to 0.1875
- w_value: bfloat16 [1024, 1024], P('dp', 'tensor'), may hold values from -0.1875 to 0.1875
- w_out: bfloat16 [1024, 1024], P('tensor', 'dp'), may hold values from -1.5 to 1.5
- w_gate: bfloat16 [4, 1024, 2816], P(None, 'dp', 'tensor'), may hold values from -0.1875 to 0.1875
- w_up: bfloat16 [4, 1024, 2816], P(None, 'dp', 'tensor'), may hold values from -0.1875 to 0.1875
- w_down: bfloat16 [4, 2816, 1024], P(None, 'tensor', 'dp'), may hold values from -0.21875 to 0.21875
- expert_ids: int32 [12288, 2], P('dp'), may hold values from 0 to 3, as said below
- priority: int32 [8, 3072], P('dp'), may hold values from 0 to 3071, each once within a row
Outputs:
- output: bfloat16 [12288, 1024], P(('dp', 'tensor'))
- input_grad: float32 [12288, 1024], P(('dp', 'tensor'))
- attn_gain_grad: float32 [1024], P(('dp', 'tensor'))
- moe_gain_grad: float32 [1024], P(('dp', 'tensor'))
- router_grad: float32 [1024, 4], P(('dp', 'tensor'))
- w_query_grad: float32 [1024, 1024], P('dp', 'tensor')
- w_key_grad: float32 [1024, 1024], P('dp', 'tensor')
- w_value_grad: float32 [1024, 1024], P('dp', 'tensor')
- w_out_grad: float32 [1024, 1024], P('tensor', 'dp')
- w_gate_grad: float32 [4, 1024, 2816], P(None, 'dp', 'tensor')
- w_up_grad: float32 [4, 1024, 2816], P(None, 'dp', 'tensor')
- w_down_grad: float32 [4, 2816, 1024], P(None, 'tensor', 'dp')
The draws below stay inside these ranges and needn't reach their ends.
Inputs may be any that keep to these rules, and one draw needn't show every extreme that they name: `expert_ids`: each row names two different experts. `priority`: each row is an ordering of the group's token-choice pairs.
All inputs are finite; a program needn't handle non-finite values.
Results may differ from the reference program's by a relative error of at most 0.024.
Values may be sent and summed in bfloat16 or wider, within the bound.
No kernel may reach another device: no remote copies, remote signals or barrier semaphores. Data moves between devices by JAX's collectives and lax.ppermute only.
A program may use at most 256 MiB of HBM per device.

```python
import jax
import jax.numpy as jnp
from jax import lax

D = 1024
HEADS = 16
HEAD_DIM = 64
FF = 2816
EXPERTS = 4
PROMPT = 1024
CONT = 128
QUERY_BLOCK = 512
GROUP_TOK = 1536
PAIRS = 3072
CAPACITY = 960
GROUPS = 8
TOKENS = 12288


def draw_expert_ids(key, part):
    key = jax.random.fold_in(key, 11)
    key_order, key_first, key_second = jax.random.split(key, 3)
    group_keys = jax.random.split(key_order, GROUPS)
    ranking = jax.vmap(lambda item: jax.random.permutation(item, EXPERTS))(group_keys)
    weights = (EXPERTS - ranking).astype(jnp.int32)
    bounds = jnp.cumsum(weights, -1)
    total = EXPERTS * (EXPERTS + 1) // 2
    first_draw = jax.random.randint(key_first, (GROUPS, GROUP_TOK), 0, total)
    first = jnp.sum((first_draw[:, :, None] >= bounds[:, None, :]).astype(jnp.int32), -1)
    picked = first[:, :, None] == jnp.arange(EXPERTS, dtype=jnp.int32)[None, None, :]
    remaining = jnp.where(picked, 0, weights[:, None, :])
    rest_bounds = jnp.cumsum(remaining, -1)
    rest_total = rest_bounds[:, :, EXPERTS - 1]
    second_draw = jax.random.randint(key_second, (GROUPS, GROUP_TOK), 0, 1 << 20) % rest_total
    second = jnp.sum((second_draw[:, :, None] >= rest_bounds).astype(jnp.int32), -1)
    return jnp.stack([first, second], -1).reshape(TOKENS, 2).astype(jnp.int32)


def levels(key, dims, cuts, smallest, largest):
    level = 1.0
    for axis_at, blocks in cuts:
        draws = jax.random.uniform(jax.random.fold_in(jax.random.fold_in(key, 6), axis_at), (blocks,), jnp.float32, smallest / len(cuts), largest / len(cuts))
        level = level * jnp.repeat(jnp.exp(draws), dims[axis_at] // blocks).reshape((-1,) + (1,) * (len(dims) - 1 - axis_at))
    return level


def noise(key, dims, deviation, bound, shards=(), held_as=jnp.bfloat16):
    entries = jax.random.normal(key, dims, jnp.float32) * deviation
    if len(shards) > 0:
        entries = levels(key, dims, shards, -0.22, 0.18) * entries
    return jnp.clip(entries, min=-bound, max=bound).astype(held_as)


def setup_inputs(seed: int = 0) -> dict:
    splits = jax.random.split(jax.random.key(seed), 15)
    inputs = noise(splits[0], (TOKENS, D), 1.0, 6.0, ((0, 32),))
    cotangent = noise(splits[1], (TOKENS, D), 1.0, 6.0, ((0, 32),))
    attn_gain = jnp.clip(1.0 + 0.1 * jax.random.normal(splits[2], (D,), jnp.float32), 0.5, 1.5).astype(jnp.bfloat16)
    moe_gain = jnp.clip(1.0 + 0.1 * jax.random.normal(splits[3], (D,), jnp.float32), 0.5, 1.5).astype(jnp.bfloat16)
    router = noise(splits[4], (D, EXPERTS), (2 * D) ** -0.5, 0.125, ((0, 32),))
    w_query = noise(splits[5], (D, D), D ** -0.5, 0.1875, ((0, 8), (1, 4)))
    w_key = noise(splits[6], (D, D), D ** -0.5, 0.1875, ((0, 8), (1, 4)))
    w_value = noise(splits[7], (D, D), D ** -0.5, 0.1875, ((0, 8), (1, 4)))
    w_out = noise(splits[8], (D, D), (D // 64) ** -0.5, 1.5, ((0, 4), (1, 8)))
    w_gate = noise(splits[9], (EXPERTS, D, FF), D ** -0.5, 0.1875, ((1, 8), (2, 4)))
    w_up = noise(splits[10], (EXPERTS, D, FF), D ** -0.5, 0.1875, ((1, 8), (2, 4)))
    w_down = noise(splits[11], (EXPERTS, FF, D), (FF // 4) ** -0.5, 0.21875, ((1, 4), (2, 8)))
    expert_ids = draw_expert_ids(jax.random.fold_in(splits[14], 71), 0)
    priority = jax.vmap(lambda own: jax.random.permutation(own, PAIRS))(jax.random.split(splits[13], GROUPS)).reshape((GROUPS, PAIRS)).astype(jnp.int32)
    return {"inputs": inputs, "cotangent": cotangent, "attn_gain": attn_gain, "moe_gain": moe_gain, "router": router, "w_query": w_query, "w_key": w_key, "w_value": w_value, "w_out": w_out, "w_gate": w_gate, "w_up": w_up, "w_down": w_down, "expert_ids": expert_ids, "priority": priority}


@jax.custom_vjp
def low(v):
    return lax.optimization_barrier(v.astype(jnp.bfloat16)).astype(jnp.float32)

@jax.custom_vjp
def low_back(v):
    return v

def low_keep(v):
    return (low(v), None)

def low_pass(kept, grad):
    return (grad,)

def back_keep(v):
    return (v, None)

def back_low(kept, grad):
    return (low(grad),)
low.defvjp(low_keep, low_pass)
low_back.defvjp(back_keep, back_low)
EPS = 1e-06
HIGH = lax.Precision.HIGHEST

def matmul(left, right):
    return jnp.dot(left, right, precision=HIGH, preferred_element_type=jnp.float32)

def rms(values, gain):
    return values * lax.rsqrt(lax.optimization_barrier(jnp.mean(values * values, -1, keepdims=True)) + EPS) * gain

def block_keys(whole, start):
    own = lax.dynamic_slice_in_dim(whole, start, QUERY_BLOCK, 0)
    return jnp.concatenate([whole[:PROMPT], own], 0)

def block_mask(start):
    rows = start + jnp.arange(QUERY_BLOCK, dtype=jnp.int32)
    cols = jnp.concatenate([jnp.arange(PROMPT, dtype=jnp.int32), start + jnp.arange(QUERY_BLOCK, dtype=jnp.int32)])
    first = jnp.arange(PROMPT + QUERY_BLOCK, dtype=jnp.int32) < PROMPT
    row_at = rows[:, None]
    col_at = cols[None, :]
    prompt_part = first[None, :] & ((row_at >= PROMPT) | (col_at <= row_at))
    same = (row_at - PROMPT) // CONT == (col_at - PROMPT) // CONT
    own_part = ~first[None, :] & (row_at >= PROMPT) & (col_at >= PROMPT) & same & (col_at <= row_at)
    return prompt_part | own_part

def assign_slots(expert_ids, priority, count, capacity):
    flat_ids = expert_ids.reshape(-1).astype(jnp.int32)
    pairs = flat_ids.shape[0]
    order = jnp.zeros((pairs,), jnp.int32).at[priority].set(jnp.arange(pairs, dtype=jnp.int32))
    sorted_ids = flat_ids[order]
    onehot = (sorted_ids[:, None] == jnp.arange(count, dtype=jnp.int32)[None, :]).astype(jnp.int32)
    ranks_sorted = lax.optimization_barrier(jnp.sum(jnp.cumsum(onehot, 0) * onehot, 1)) - 1
    ranks = ranks_sorted[priority]
    kept = ranks < capacity
    slot = flat_ids * capacity + jnp.minimum(ranks, capacity - 1)
    target = jnp.where(kept, flat_ids * capacity + ranks, count * capacity)
    owner = jnp.full((count * capacity + 1,), pairs, jnp.int32).at[target].set(jnp.arange(pairs, dtype=jnp.int32))
    return (kept, slot, owner[:count * capacity])

def group_layer(params, rows, expert_ids, priority):
    attn_gain, moe_gain, router, wq, wk, wv, wo, wg, wu, wd = params
    normed = low(rms(rows, attn_gain))

    def project(weight):
        return low(low_back(matmul(normed, weight))).reshape(GROUP_TOK, HEADS, HEAD_DIM)
    queries, keys_all, values_all = (project(wq), project(wk), project(wv))

    def one_block(start):
        q_blk = lax.dynamic_slice_in_dim(queries, start, QUERY_BLOCK, 0)
        keys = block_keys(keys_all, start)
        vals = block_keys(values_all, start)
        scores = low_back(jnp.einsum('qhd,khd->hqk', q_blk, keys, precision=HIGH) * 0.125)
        scores = jnp.where(block_mask(start)[None], scores, -1e+30)
        probs = low(jax.nn.softmax(scores, axis=-1))
        return jnp.einsum('hqk,khd->qhd', probs, vals, precision=HIGH).reshape(QUERY_BLOCK, D)
    starts = jnp.arange(GROUP_TOK // QUERY_BLOCK, dtype=jnp.int32) * QUERY_BLOCK
    context = low(low_back(lax.map(jax.checkpoint(one_block), starts).reshape(GROUP_TOK, D)))
    middle = rows + low_back(matmul(context, wo))
    mixed = low(rms(middle, moe_gain))
    route = jax.nn.softmax(matmul(mixed, router), axis=-1)
    choose = (expert_ids[:, :, None] == jnp.arange(EXPERTS, dtype=jnp.int32)[None, None, :]).astype(jnp.float32)
    gates = low(lax.optimization_barrier(jnp.sum(route[:, None, :] * choose, -1))).reshape(-1)
    kept, slot, owner = assign_slots(expert_ids, priority, EXPERTS, CAPACITY)
    filled = (owner < PAIRS).astype(jnp.float32)
    token = jnp.minimum(owner, PAIRS - 1) // 2
    xin = (mixed[token] * filled[:, None]).reshape(EXPERTS, CAPACITY, D)
    gate_pre = low_back(jnp.einsum('ecd,edf->ecf', xin, wg, precision=HIGH))
    up_pre = low_back(jnp.einsum('ecd,edf->ecf', xin, wu, precision=HIGH))
    hidden = low(jax.nn.gelu(gate_pre, approximate=False) * up_pre)
    expert_out = low_back(jnp.einsum('ecf,efd->ecd', hidden, wd, precision=HIGH)).reshape(EXPERTS * CAPACITY, D)
    weight = kept.astype(jnp.float32) * gates
    combined = lax.optimization_barrier(jnp.sum((expert_out[slot] * weight[:, None]).reshape(GROUP_TOK, 2, D), 1))
    return middle + combined

def reference(inputs, cotangent, attn_gain, moe_gain, router, w_query, w_key, w_value, w_out, w_gate, w_up, w_down, expert_ids, priority):
    floats = tuple((item.astype(jnp.float32) for item in (inputs, attn_gain, moe_gain, router, w_query, w_key, w_value, w_out, w_gate, w_up, w_down)))
    group_ids = expert_ids.reshape(GROUPS, GROUP_TOK, 2)

    def whole(rows, *params):
        stacked = rows.reshape(GROUPS, GROUP_TOK, D)
        layer = jax.checkpoint(group_layer)

        def one_group(items):
            return layer(params, items[0], items[1], items[2])
        return lax.map(one_group, (stacked, group_ids, priority)).reshape(TOKENS, D)
    result, pull = jax.vjp(whole, *floats)
    grads = pull(cotangent.astype(jnp.float32))
    return (result.astype(jnp.bfloat16), grads[0], grads[1], grads[2], grads[3], grads[4], grads[5], grads[6], grads[7], grads[8], grads[9], grads[10])
```

```python
import jax
import jax.numpy as jnp
from jax import lax
from jax.experimental import pallas as pl
from jax.experimental.pallas import tpu as pltpu
from jax.sharding import PartitionSpec as P

HEAD_DIM = 64
PROMPT = 1024
CONT = 128
CAPACITY = 960
EPS = 1e-06
PAIR = 2 * HEAD_DIM
MIB = 2**20

f32 = jnp.float32
b16 = jnp.bfloat16
NN = (((1,), (0,)), ((), ()))
NT = (((1,), (1,)), ((), ()))
TN = (((0,), (0,)), ((), ()))
INV_SQRT2 = 0.7071067811865476
INV_SQRT_2PI = 0.3989422804014327
MASKED = -1e30


def dot(left, right, dims):
    return lax.dot_general(left, right, dims, preferred_element_type=f32)


def params(mib):
    return pltpu.CompilerParams(vmem_limit_bytes=mib * MIB)


def whole(*_):
    return (0, 0)


def unit_of(values):
    scale = lax.rsqrt(jnp.mean(values * values, -1, keepdims=True) + EPS)
    return values * scale, scale


def keep_mask(ids, order, experts):
    rows = ids.shape[1]
    pairs = ids.shape[0] * rows
    bits = pairs.bit_length()

    def body(ids_ref, order_ref, keep_ref):
        ids_v = ids_ref[...]
        order_v = order_ref[...]
        sub = lax.broadcasted_iota(jnp.int32, (128, rows), 0)
        out = jnp.zeros((128, rows), f32)
        for expert in range(experts):
            mine = ids_v == expert
            bound = jnp.zeros((1, 1), jnp.int32)
            for bit in range(bits - 1, -1, -1):
                trial = bound + (1 << bit)
                inside = jnp.where(mine & (order_v < trial), 1.0, 0.0)
                count = jnp.sum(jnp.sum(inside, 1, keepdims=True), 0, keepdims=True)
                bound = jnp.where(count <= CAPACITY, trial, bound)
            kept = jnp.sum(jnp.where(mine & (order_v < bound), 1.0, 0.0), 0, keepdims=True)
            out = jnp.where((sub < 2 * experts) & (sub % experts == expert), kept, out)
        keep_ref[...] = jnp.transpose(out)

    return pl.pallas_call(
        body,
        out_shape=jax.ShapeDtypeStruct((rows, 128), f32),
        compiler_params=params(32),
    )(ids, order)


def attention_forward(at, slots, gains, weights):
    rows, width = slots[0].shape
    groups, _, _, cols = weights.shape
    tall = PROMPT + rows
    subs = rows // CONT
    pairs = cols // PAIR
    keys = PROMPT + CONT

    def body(at_ref, x0, x1, x2, x3, gain_ref, w_ref, a_ref, q_ref, k_ref, v_ref, p_ref, c_ref, h_ref, b_ref, xs, acc):
        step = pl.program_id(0)
        t = at_ref[0]

        @pl.when(step == 0)
        def _():
            for s, x in enumerate((x0, x1, x2, x3)):
                xs[s * rows : (s + 1) * rows] = x[...]
            gain = gain_ref[0:1]
            for start in range(0, PROMPT, rows):
                take = min(rows, PROMPT - start)
                slot = jnp.maximum(t - start // rows, 0)
                x = xs[pl.ds(pl.multiple_of(slot * rows, 128), take)].astype(f32)
                a_ref[start : start + take] = (unit_of(x)[0] * gain).astype(b16)
            a_ref[PROMPT:tall] = (unit_of(x0[...].astype(f32))[0] * gain).astype(b16)

        a = a_ref[...]
        q = dot(a_ref[PROMPT:tall], w_ref[0, 0], NN).astype(b16) * jnp.asarray(0.125, b16)
        k = dot(a, w_ref[0, 1], NN).astype(b16)
        v = dot(a, w_ref[0, 2], NN).astype(b16)
        q_ref[...] = q
        k_ref[...] = k
        v_ref[...] = v
        low = lax.broadcasted_iota(jnp.int32, (CONT, PAIR), 1) < HEAD_DIM
        row = lax.broadcasted_iota(jnp.int32, (2 * CONT, PROMPT), 0) % CONT
        col = lax.broadcasted_iota(jnp.int32, (2 * CONT, PROMPT), 1)
        own_ok = lax.broadcasted_iota(jnp.int32, (2 * CONT, CONT), 1) <= (
            lax.broadcasted_iota(jnp.int32, (2 * CONT, CONT), 0) % CONT
        )
        zero = jnp.zeros((), b16)
        for pair in range(pairs):
            lanes = slice(pair * PAIR, (pair + 1) * PAIR)
            kp, vp = k[:PROMPT, lanes], v[:PROMPT, lanes]
            for sub in range(subs):
                own = slice(PROMPT + sub * CONT, PROMPT + (sub + 1) * CONT)
                q2 = q[sub * CONT : (sub + 1) * CONT, lanes]
                qs = jnp.concatenate([jnp.where(low, q2, zero), jnp.where(low, zero, q2)], 0)
                first = t * rows + sub * CONT
                s1 = jnp.where(col <= row + first, dot(qs, kp, NT), MASKED)
                s2 = jnp.where(own_ok & (first >= PROMPT), dot(qs, k[own, lanes], NT), MASKED)
                top = jnp.maximum(jnp.max(s1, -1, keepdims=True), jnp.max(s2, -1, keepdims=True))
                e1 = jnp.exp(s1 - top)
                e2 = jnp.exp(s2 - top)
                inv = 1.0 / (jnp.sum(e1, -1, keepdims=True) + jnp.sum(e2, -1, keepdims=True))
                p1 = (e1 * inv).astype(b16)
                p2 = (e2 * inv).astype(b16)
                at_p = slice((pair * subs + sub) * 2 * CONT, (pair * subs + sub + 1) * 2 * CONT)
                p_ref[0, at_p, :PROMPT] = p1
                p_ref[0, at_p, PROMPT:] = p2
                c2 = dot(p1, vp, NN) + dot(p2, v[own, lanes], NN)
                c_ref[sub * CONT : (sub + 1) * CONT, lanes] = jnp.where(low, c2[:CONT], c2[CONT:]).astype(b16)
        out = dot(c_ref[...], w_ref[0, 3], NT)

        @pl.when(step == 0)
        def _():
            acc[...] = out

        @pl.when(step > 0)
        def _():
            acc[...] += out

        @pl.when(step == groups - 1)
        def _():
            h = x0[...].astype(f32) + acc[...]
            h_ref[...] = h
            b_ref[...] = (unit_of(h)[0] * gain_ref[1:2]).astype(b16)

    def by_group(i, at):
        return (0, i)

    return pl.pallas_call(
        body,
        grid_spec=pltpu.PrefetchScalarGridSpec(
            num_scalar_prefetch=1,
            grid=(groups,),
            in_specs=[pl.BlockSpec((rows, width), whole)] * 4
            + [
                pl.BlockSpec(gains.shape, whole),
                pl.BlockSpec((1, 4, width, cols), lambda i, at: (i, 0, 0, 0)),
            ],
            out_specs=[
                pl.BlockSpec((tall, width), whole),
                pl.BlockSpec((rows, cols), by_group),
                pl.BlockSpec((tall, cols), by_group),
                pl.BlockSpec((tall, cols), by_group),
                pl.BlockSpec((1, 2 * pairs * rows, keys), lambda i, at: (i, 0, 0)),
                pl.BlockSpec((rows, cols), by_group),
                pl.BlockSpec((rows, width), whole),
                pl.BlockSpec((rows, width), whole),
            ],
            scratch_shapes=[pltpu.VMEM((4 * rows, width), b16), pltpu.VMEM((rows, width), f32)],
        ),
        out_shape=[
            jax.ShapeDtypeStruct((tall, width), b16),
            jax.ShapeDtypeStruct((rows, width), b16),
            jax.ShapeDtypeStruct((tall, width), b16),
            jax.ShapeDtypeStruct((tall, width), b16),
            jax.ShapeDtypeStruct((groups, 2 * pairs * rows, keys), b16),
            jax.ShapeDtypeStruct((rows, width), b16),
            jax.ShapeDtypeStruct((rows, width), f32),
            jax.ShapeDtypeStruct((rows, width), b16),
        ],
        compiler_params=params(56),
        cost_estimate=pl.CostEstimate(
            flops=2 * width * width * (2 * tall + 2 * rows) + 8 * rows * keys * width,
            bytes_accessed=60 * MIB,
            transcendentals=rows * keys * 16,
        ),
    )(at, *slots, gains, weights)


def attention_backward(at, h, dy, parts, gains, a, q, k, v, p, c, weights):
    rows, width = h.shape
    groups, _, _, cols = weights.shape
    tall = PROMPT + rows
    padded = -(-PROMPT // rows) * rows
    subs = rows // CONT
    pairs = cols // PAIR
    keys = PROMPT + CONT

    def body(at_ref, h_ref, dy_ref, d0, d1, d2, d3, gain_ref, a_ref, q_ref, k_ref, v_ref, p_ref, c_ref, w_ref, dw_ref, dap_ref, dao_ref, dh_ref, sum_ref, do, acc, ds, dqs):
        step = pl.program_id(0)

        @pl.when(step == 0)
        def _():
            dn = (d0[...].astype(f32) + d1[...].astype(f32)) + (d2[...].astype(f32) + d3[...].astype(f32))
            gain = gain_ref[1:2]
            unit, scale = unit_of(h_ref[...])
            along = dn * gain
            inner = jnp.mean(along * unit, -1, keepdims=True)
            dh = dy_ref[...].astype(f32) + scale * (along - unit * inner)
            dh_ref[...] = dh
            do[...] = dh.astype(b16)
            sum_ref[...] = jnp.zeros_like(sum_ref)
            sum_ref[1:2] = jnp.sum(dn * unit, 0, keepdims=True)

        low = lax.broadcasted_iota(jnp.int32, (CONT, PAIR), 1) < HEAD_DIM
        zero = jnp.zeros((), b16)

        def stacked(two):
            return jnp.concatenate([jnp.where(low, two, zero), jnp.where(low, zero, two)], 0)

        dc = dot(do[...], w_ref[0, 3], NN).astype(b16)
        dw_ref[0, 3] = dot(do[...], c_ref[...], TN).astype(b16)
        dks, dvs = [], []
        for pair in range(pairs):
            lanes = slice(pair * PAIR, (pair + 1) * PAIR)
            kp, vp = k_ref[:PROMPT, lanes], v_ref[:PROMPT, lanes]
            qall, dcall, dko, dvo = [], [], [], []
            for sub in range(subs):
                own = slice(PROMPT + sub * CONT, PROMPT + (sub + 1) * CONT)
                mine = slice(sub * CONT, (sub + 1) * CONT)
                at_p = slice((pair * subs + sub) * 2 * CONT, (pair * subs + sub + 1) * 2 * CONT)
                dcs = stacked(dc[mine, lanes])
                qs = stacked(q_ref[mine, lanes])
                cs = stacked(c_ref[mine, lanes])
                delta = jnp.sum(dcs.astype(f32) * cs.astype(f32), -1, keepdims=True)
                p1 = p_ref[0, at_p, :PROMPT]
                p2 = p_ref[0, at_p, PROMPT:]
                ds1 = (p1.astype(f32) * (dot(dcs, vp, NT) - delta)).astype(b16)
                ds2 = (p2.astype(f32) * (dot(dcs, v_ref[own, lanes], NT) - delta)).astype(b16)
                ds[sub * 2 * CONT : (sub + 1) * 2 * CONT] = ds1
                dq2 = (dot(ds1, kp, NN) + dot(ds2, k_ref[own, lanes], NN)) * 0.125
                dqs[mine, lanes] = jnp.where(low, dq2[:CONT], dq2[CONT:]).astype(b16)
                dko.append(dot(ds2, qs, TN).astype(b16))
                dvo.append(dot(p2, dcs, TN).astype(b16))
                qall.append(qs)
                dcall.append(dcs)
            span = slice(pair * 2 * rows, (pair + 1) * 2 * rows)
            dkp = dot(ds[...], jnp.concatenate(qall, 0), TN).astype(b16)
            dvp = dot(p_ref[0, span, :PROMPT], jnp.concatenate(dcall, 0), TN).astype(b16)
            dks.append(jnp.concatenate([dkp] + dko, 0))
            dvs.append(jnp.concatenate([dvp] + dvo, 0))
        dk = jnp.concatenate(dks, 1)
        dv = jnp.concatenate(dvs, 1)
        dq = dqs[...]
        dw_ref[0, 0] = dot(a_ref[PROMPT:tall], dq, TN).astype(b16)
        dw_ref[0, 1] = dot(a_ref[...], dk, TN).astype(b16)
        dw_ref[0, 2] = dot(a_ref[...], dv, TN).astype(b16)
        terms = dot(dk, w_ref[0, 1], NT) + dot(dv, w_ref[0, 2], NT)
        own_terms = terms[PROMPT:] + dot(dq, w_ref[0, 0], NT)

        @pl.when(step == 0)
        def _():
            acc[:PROMPT] = terms[:PROMPT]
            acc[PROMPT:] = own_terms

        @pl.when(step > 0)
        def _():
            acc[:PROMPT] += terms[:PROMPT]
            acc[PROMPT:] += own_terms

        @pl.when(step == groups - 1)
        def _():
            dap_ref[:PROMPT] = acc[:PROMPT].astype(b16)
            if padded > PROMPT:
                dap_ref[PROMPT:] = jnp.zeros((padded - PROMPT, width), b16)
            dao_ref[...] = acc[PROMPT:]
            total = jnp.sum(acc[...] * a_ref[...].astype(f32), 0, keepdims=True)
            sum_ref[0:1] = total / gain_ref[0:1]

    def by_group(i, at):
        return (0, i)

    return pl.pallas_call(
        body,
        grid_spec=pltpu.PrefetchScalarGridSpec(
            num_scalar_prefetch=1,
            grid=(groups,),
            in_specs=[pl.BlockSpec((rows, width), whole)] * 6
            + [
                pl.BlockSpec(gains.shape, whole),
                pl.BlockSpec((tall, width), whole),
                pl.BlockSpec((rows, cols), by_group),
                pl.BlockSpec((tall, cols), by_group),
                pl.BlockSpec((tall, cols), by_group),
                pl.BlockSpec((1, 2 * pairs * rows, keys), lambda i, at: (i, 0, 0)),
                pl.BlockSpec((rows, cols), by_group),
                pl.BlockSpec((1, 4, width, cols), lambda i, at: (i, 0, 0, 0)),
            ],
            out_specs=[
                pl.BlockSpec((1, 4, width, cols), lambda i, at: (i, 0, 0, 0)),
                pl.BlockSpec((padded, width), whole),
                pl.BlockSpec((rows, width), whole),
                pl.BlockSpec((rows, width), whole),
                pl.BlockSpec((8, width), whole),
            ],
            scratch_shapes=[
                pltpu.VMEM((rows, width), b16),
                pltpu.VMEM((tall, width), f32),
                pltpu.VMEM((2 * rows, PROMPT), b16),
                pltpu.VMEM((rows, cols), b16),
            ],
        ),
        out_shape=[
            jax.ShapeDtypeStruct(weights.shape, b16),
            jax.ShapeDtypeStruct((padded, width), b16),
            jax.ShapeDtypeStruct((rows, width), f32),
            jax.ShapeDtypeStruct((rows, width), f32),
            jax.ShapeDtypeStruct((8, width), f32),
        ],
        compiler_params=params(60),
        cost_estimate=pl.CostEstimate(
            flops=4 * width * width * (2 * tall + 2 * rows) + 16 * rows * keys * width,
            bytes_accessed=80 * MIB,
            transcendentals=0,
        ),
    )(at, h, dy, *parts, gains, a, q, k, v, p, c, weights)


def experts_block(block, b, dy, keep, router, wg, wu, wd, experts):
    rows, width = b.shape
    units = wg.shape[0]
    own = units // experts
    chunk = 256
    steps = units // chunk

    def body(block_ref, b_ref, dy_ref, keep_ref, r_ref, wg_ref, wu_ref, wd_ref, y_ref, db_ref, rg_ref, z_ref, dg_ref, du_ref, gates, probs, dgates, y_acc, db_acc):
        i = pl.program_id(0)
        lane = lax.broadcasted_iota(jnp.int32, (rows, 128), 1)
        b_v = b_ref[...]
        dy_v = dy_ref[...]

        @pl.when(i == 0)
        def _():
            logits = dot(b_v, r_ref[...], NN)
            live = lane < experts
            top = jnp.max(jnp.where(live, logits, MASKED), -1, keepdims=True)
            grown = jnp.exp(jnp.where(lane < 2 * experts, logits, MASKED) - top)
            share = grown / jnp.sum(jnp.where(live, grown, 0.0), -1, keepdims=True)
            probs[...] = share
            gates[...] = share.astype(b16).astype(f32) * keep_ref[...]
            dgates[...] = jnp.zeros_like(dgates)

        g = dot(b_v, wg_ref[...], NT)
        u = dot(b_v, wu_ref[...], NT)
        dz_plain = dot(dy_v, wd_ref[...], NT)
        first = (i * chunk) // own
        last = (i * chunk + chunk - 1) // own
        gate_v = gates[...]
        gate_a = jnp.sum(jnp.where(lane == first, gate_v, 0.0), -1, keepdims=True)
        gate_b = jnp.sum(jnp.where(lane == last, gate_v, 0.0), -1, keepdims=True)
        is_a = lax.broadcasted_iota(jnp.int32, (rows, chunk), 1) < (first + 1) * own - i * chunk
        gate = jnp.where(is_a, gate_a, gate_b)
        cdf = 0.5 * (1.0 + lax.erf(g * INV_SQRT2))
        act = g * cdf
        z = (act * u).astype(b16).astype(f32)
        along = dz_plain * z
        all_sum = jnp.sum(along, -1, keepdims=True)
        a_sum = jnp.sum(jnp.where(is_a, along, 0.0), -1, keepdims=True)
        dgates[...] += jnp.where(lane % experts == first, a_sum, 0.0) + jnp.where(lane % experts == last, all_sum - a_sum, 0.0)
        dz = dz_plain * gate
        pdf = INV_SQRT_2PI * jnp.exp(-0.5 * g * g)
        dg = (dz * u * (cdf + g * pdf)).astype(b16)
        du = (dz * act).astype(b16)
        zg = (z * gate).astype(b16)
        z_ref[...] = zg
        dg_ref[...] = dg
        du_ref[...] = du
        y = dot(zg, wd_ref[...], NN)
        db = dot(dg, wg_ref[...], NN) + dot(du, wu_ref[...], NN)

        @pl.when(i == 0)
        def _():
            y_acc[...] = y
            db_acc[...] = db

        @pl.when(i > 0)
        def _():
            y_acc[...] += y
            db_acc[...] += db

        @pl.when(i == steps - 1)
        def _():
            share = probs[...]
            dprob = dgates[...] * keep_ref[...]
            inner = jnp.sum(jnp.where(lane < experts, share * dprob, 0.0), -1, keepdims=True)
            dl = jnp.where(lane < 2 * experts, share * (dprob - inner), 0.0)
            head = dl.astype(b16).astype(f32)
            split = jnp.where(lane < experts, head, dl - head).astype(b16)
            rg_ref[...] = dot(b_v, split, TN)
            y_ref[...] = y_acc[...].astype(b16)
            db_ref[...] = (db_acc[...] + dot(split, r_ref[...], NT)).astype(b16)

    weight = pl.BlockSpec((chunk, width), lambda i, at: (i, 0))
    hidden = pl.BlockSpec((rows, chunk), lambda i, at: (0, i))
    return pl.pallas_call(
        body,
        grid_spec=pltpu.PrefetchScalarGridSpec(
            num_scalar_prefetch=1,
            grid=(steps,),
            in_specs=[
                pl.BlockSpec((rows, width), whole),
                pl.BlockSpec((rows, width), whole),
                pl.BlockSpec((rows, 128), lambda i, at: (at[0], 0)),
                pl.BlockSpec((width, 128), whole),
                weight,
                weight,
                weight,
            ],
            out_specs=[
                pl.BlockSpec((rows, width), whole),
                pl.BlockSpec((rows, width), whole),
                pl.BlockSpec((width, 128), whole),
                hidden,
                hidden,
                hidden,
            ],
            scratch_shapes=[pltpu.VMEM((rows, 128), f32)] * 3 + [pltpu.VMEM((rows, width), f32)] * 2,
        ),
        out_shape=[
            jax.ShapeDtypeStruct((rows, width), b16),
            jax.ShapeDtypeStruct((rows, width), b16),
            jax.ShapeDtypeStruct((width, 128), f32),
        ]
        + [jax.ShapeDtypeStruct((rows, units), b16)] * 3,
        compiler_params=params(48),
        cost_estimate=pl.CostEstimate(
            flops=12 * rows * width * units,
            bytes_accessed=6 * units * width + 6 * rows * units,
            transcendentals=2 * rows * units,
        ),
    )(block, b, dy, keep, router, wg, wu, wd)


def experts_weights(bs, dys, zs, dgs, dus, parts):
    slots = len(bs)
    rows, width = bs[0].shape
    units = zs[0].shape[1]
    chunk = 256
    cut = width // parts

    def body(*refs):
        b_refs, dy_refs, z, dg, du = (refs[n * slots : (n + 1) * slots] for n in range(5))
        out_g, out_u, out_d, b_all, dy_all = refs[5 * slots :]

        @pl.when(pl.program_id(0) == 0)
        def _():
            for s in range(slots):
                b_all[s * rows : (s + 1) * rows] = b_refs[s][...]
                dy_all[s * rows : (s + 1) * rows] = dy_refs[s][...]

        for left, right, out in ((dg, b_all, out_g), (du, b_all, out_u), (z, dy_all, out_d)):
            joined = jnp.concatenate([r[...] for r in left], 0)
            value = dot(joined, right[...], TN).astype(b16)
            if parts == 1:
                out[...] = value
            else:
                for part in range(parts):
                    out[part] = value[:, part * cut : (part + 1) * cut]

    if parts == 1:
        spec = pl.BlockSpec((chunk, width), lambda i: (i, 0))
        shape = jax.ShapeDtypeStruct((units, width), b16)
    else:
        spec = pl.BlockSpec((parts, chunk, cut), lambda i: (0, i, 0))
        shape = jax.ShapeDtypeStruct((parts, units, cut), b16)
    return pl.pallas_call(
        body,
        grid=(units // chunk,),
        in_specs=[pl.BlockSpec((rows, width), whole)] * (2 * slots)
        + [pl.BlockSpec((rows, chunk), lambda i: (0, i))] * (3 * slots),
        out_specs=[spec] * 3,
        out_shape=[shape] * 3,
        scratch_shapes=[pltpu.VMEM((slots * rows, width), b16)] * 2,
        compiler_params=params(48),
        cost_estimate=pl.CostEstimate(
            flops=6 * slots * rows * width * units,
            bytes_accessed=6 * units * width + 6 * slots * rows * units,
            transcendentals=0,
        ),
    )(*bs, *dys, *zs, *dgs, *dus)


def input_gradient(dh, own, piece, sent, x, gains):
    rows, width = dh.shape

    def body(dh_ref, own_ref, piece_ref, sent_ref, x_ref, gain_ref, out_ref):
        da = own_ref[...] + (piece_ref[...].astype(f32) + sent_ref[...].astype(f32))
        unit, scale = unit_of(x_ref[...].astype(f32))
        along = da * gain_ref[0:1]
        inner = jnp.mean(along * unit, -1, keepdims=True)
        out_ref[...] = dh_ref[...] + scale * (along - unit * inner)

    block = pl.BlockSpec((CONT, width), lambda i: (i, 0))
    return pl.pallas_call(
        body,
        grid=(rows // CONT,),
        in_specs=[block] * 5 + [pl.BlockSpec(gains.shape, whole)],
        out_specs=block,
        out_shape=jax.ShapeDtypeStruct((rows, width), f32),
        compiler_params=params(32),
    )(dh, own, piece, sent, x, gains)


def on_device(inputs, cotangent, attn_gain, moe_gain, router, w_query, w_key, w_value, w_out, w_gate, w_up, w_down, expert_ids, priority):
    rows, width = inputs.shape
    experts, cut, own_units = w_gate.shape
    units = experts * own_units
    dp = lax.axis_size("dp")
    depth = lax.axis_size("tensor")
    own = lax.axis_index("tensor")
    at = jnp.full((1,), own, jnp.int32)
    up = [(i, i + 1) for i in range(depth - 1)]
    down = [(i + 1, i) for i in range(depth - 1)]

    def swap(value, bits):
        return lax.ppermute(value, "tensor", [(i, i ^ bits) for i in range(depth)])

    mine = jnp.stack([w_query, w_key, w_value, w_out.T])
    near = swap(mine, 1)
    far = swap(mine, 2)
    attention_w = lax.all_gather(jnp.stack([mine, near, far, swap(far, 1)]), "dp", axis=2, tiled=True)

    x1 = lax.ppermute(inputs, "tensor", up)
    x2 = lax.ppermute(x1, "tensor", up)
    x3 = lax.ppermute(x2, "tensor", up)

    small = jnp.concatenate([attn_gain[:, None], moe_gain[:, None], router], 1)
    small = lax.all_gather(lax.all_gather(small, "tensor", axis=0, tiled=True), "dp", axis=0, tiled=True)
    gains = jnp.concatenate([small[:, :2].T.astype(f32), jnp.zeros((6, width), f32)], 0)
    router_full = small[:, 2:]
    router_wide = jnp.concatenate(
        [router_full, router_full, jnp.zeros((width, 128 - 2 * experts), b16)], 1
    )
    keep = keep_mask(expert_ids.T, priority.reshape(-1, 2).T, experts)

    def gather_units(shard):
        return lax.all_gather(shard.reshape(units, cut), "dp", axis=1, tiled=True)

    wg = gather_units(w_gate.transpose(0, 2, 1))
    wu = gather_units(w_up.transpose(0, 2, 1))
    wd = gather_units(w_down)

    a, q, k, v, p, c, h, b = attention_forward(at, (inputs, x1, x2, x3), gains, attention_w)

    dy2 = swap(cotangent, 2)
    dys = (cotangent, swap(cotangent, 1), dy2, swap(dy2, 1))
    b2 = swap(b, 2)
    bs = (b, swap(b, 1), b2, swap(b2, 1))
    outs = [
        experts_block(jnp.full((1,), own ^ s, jnp.int32), bs[s], dys[s], keep, router_wide, wg, wu, wd, experts)
        for s in range(depth)
    ]
    ys, dbs, rgs, zs, dgs, dus = zip(*outs)
    parts = [dbs[0]] + [swap(dbs[s], s) for s in range(1, depth)]
    y_parts = [ys[0]] + [swap(ys[s], s) for s in range(1, depth)]
    blocked = cut % 128 == 0
    grads = experts_weights(bs, dys, zs, dgs, dus, dp if blocked else 1)

    def scatter_units(grad):
        if blocked:
            total = lax.psum_scatter(grad, "dp", scatter_dimension=0, tiled=True)
        else:
            total = lax.psum_scatter(grad, "dp", scatter_dimension=1, tiled=True)
        return total.reshape(experts, own_units, cut).astype(f32)

    wg_grad, wu_grad, wd_grad = (scatter_units(grad) for grad in grads)

    dw, dap, dao, dh, sums = attention_backward(at, h, cotangent, parts, gains, a, q, k, v, p, c, attention_w)
    output = h
    for part in y_parts:
        output = output + part.astype(f32)

    def chunk_of(index):
        start = jnp.clip(index, 0, dap.shape[0] // rows - 1) * rows
        piece = lax.dynamic_slice_in_dim(dap, start, rows, 0)
        valid = (index >= 0) & (index < dap.shape[0] // rows)
        return jnp.where(valid, piece, jnp.zeros((), b16))

    sent = None
    for hop in range(1, depth):
        piece = chunk_of(own - depth + hop)
        sent = lax.ppermute(piece if sent is None else piece + sent, "tensor", down)
    input_grad = input_gradient(dh, dao, chunk_of(own), sent, inputs, gains)

    dw = lax.psum_scatter(dw, "dp", scatter_dimension=2, tiled=True)
    total = dw[0].astype(f32)
    for s in range(1, depth):
        total = total + swap(dw[s], s).astype(f32)

    rg = rgs[0] + rgs[1] + rgs[2] + rgs[3]
    small_grad = jnp.concatenate([sums[:2].T, rg[:, :experts] + rg[:, experts : 2 * experts]], 1)
    small_grad = small_grad.reshape(dp, depth, width // (dp * depth), 2 + experts)
    small_grad = lax.psum_scatter(small_grad, "tensor", scatter_dimension=1, tiled=True)
    small_grad = lax.psum_scatter(small_grad, "dp", scatter_dimension=0, tiled=True)[0, 0]
    return (
        output.astype(b16),
        input_grad,
        small_grad[:, 0],
        small_grad[:, 1],
        small_grad[:, 2:],
        total[0],
        total[1],
        total[2],
        total[3].T,
        wg_grad.transpose(0, 2, 1),
        wu_grad.transpose(0, 2, 1),
        wd_grad,
    )


def solution(mesh):
    tokens = P(("dp", "tensor"), None)
    vector = P(("dp", "tensor"))
    return jax.shard_map(
        on_device,
        mesh=mesh,
        in_specs=(tokens, tokens, vector, vector, tokens)
        + (P("dp", "tensor"),) * 3
        + (P("tensor", "dp"), P(None, "dp", "tensor"), P(None, "dp", "tensor"), P(None, "tensor", "dp"))
        + (P("dp", None), P("dp", None)),
        out_specs=(tokens, tokens, vector, vector, tokens)
        + (P("dp", "tensor"),) * 3
        + (P("tensor", "dp"), P(None, "dp", "tensor"), P(None, "dp", "tensor"), P(None, "tensor", "dp")),
        check_vma=False,
    )
```

```python
import jax
import jax.numpy as jnp
from jax import lax
from jax.experimental import pallas as pl
from jax.experimental.pallas import tpu as pltpu
from jax.sharding import PartitionSpec as P

HEAD_DIM = 64
PROMPT = 1024
CONT = 128
CAPACITY = 960
EPS = 1e-06
PAIR = 2 * HEAD_DIM
MIB = 2**20

f32 = jnp.float32
b16 = jnp.bfloat16
NN = (((1,), (0,)), ((), ()))
NT = (((1,), (1,)), ((), ()))
TN = (((0,), (0,)), ((), ()))
INV_SQRT2 = 0.7071067811865476
INV_SQRT_2PI = 0.3989422804014327
MASKED = -1e30
UNIT_CHUNK = 256
ESTIMATE = 4
FIRST_CHUNKS = 6


def dot(left, right, dims):
    return lax.dot_general(left, right, dims, preferred_element_type=f32)


def params(mib):
    return pltpu.CompilerParams(vmem_limit_bytes=mib * MIB)


def whole(*_):
    return (0, 0)


def unit_of(values):
    scale = lax.rsqrt(jnp.mean(values * values, -1, keepdims=True) + EPS)
    return values * scale, scale


def normal(v):
    bell = jnp.exp(-0.5 * v * v)
    t = 1.0 / (1.0 + (0.3275911 * INV_SQRT2) * jnp.abs(v))
    poly = t * (0.127414796 + t * (-0.142248368 + t * (0.710706871 + t * (-0.726576014 + t * 0.530702715))))
    tail = poly * bell
    return jnp.where(v < 0.0, tail, 1.0 - tail), INV_SQRT_2PI * bell


def keep_mask(ids, order, experts):
    rows = ids.shape[1]
    pairs = ids.shape[0] * rows
    bits = pairs.bit_length()

    def body(ids_ref, order_ref, keep_ref):
        ids_v = ids_ref[...]
        order_v = order_ref[...]
        sub = lax.broadcasted_iota(jnp.int32, (128, rows), 0)
        out = jnp.zeros((128, rows), f32)
        for expert in range(experts):
            mine = ids_v == expert
            bound = jnp.zeros((1, 1), jnp.int32)
            for bit in range(bits - 1, -1, -1):
                trial = bound + (1 << bit)
                inside = jnp.where(mine & (order_v < trial), 1.0, 0.0)
                count = jnp.sum(jnp.sum(inside, 1, keepdims=True), 0, keepdims=True)
                bound = jnp.where(count <= CAPACITY, trial, bound)
            kept = jnp.sum(jnp.where(mine & (order_v < bound), 1.0, 0.0), 0, keepdims=True)
            out = jnp.where((sub < 2 * experts) & (sub % experts == expert), kept, out)
        keep_ref[...] = jnp.transpose(out)

    return pl.pallas_call(
        body,
        out_shape=jax.ShapeDtypeStruct((rows, 128), f32),
        compiler_params=params(32),
    )(ids, order)


def attention_forward(at, slots, gains, weights):
    rows, width = slots[0].shape
    groups, _, _, cols = weights.shape
    tall = PROMPT + rows
    subs = rows // CONT
    pairs = cols // PAIR
    keys = PROMPT + CONT

    def body(at_ref, x0, x1, x2, x3, gain_ref, w_ref, a_ref, q_ref, k_ref, v_ref, p_ref, inv_ref, c_ref, h_ref, b_ref, xs, acc):
        step = pl.program_id(0)
        t = at_ref[0]

        @pl.when(step == 0)
        def _():
            for s, x in enumerate((x0, x1, x2, x3)):
                xs[s * rows : (s + 1) * rows] = x[...]
            gain = gain_ref[0:1]
            for start in range(0, PROMPT, rows):
                take = min(rows, PROMPT - start)
                slot = jnp.maximum(t - start // rows, 0)
                x = xs[pl.ds(pl.multiple_of(slot * rows, 128), take)].astype(f32)
                a_ref[start : start + take] = (unit_of(x)[0] * gain).astype(b16)
            x = x0[...].astype(f32)
            a_ref[PROMPT:tall] = (unit_of(x)[0] * gain).astype(b16)
            acc[...] = x

        q = dot(a_ref[PROMPT:tall], w_ref[0, 0], NN).astype(b16) * jnp.asarray(0.125, b16)
        kv = dot(a_ref[...], jnp.concatenate([w_ref[0, 1], w_ref[0, 2]], 1), NN).astype(b16)
        k, v = kv[:, :cols], kv[:, cols:]
        q_ref[...] = q
        k_ref[...] = k
        v_ref[...] = v
        low = lax.broadcasted_iota(jnp.int32, (CONT, PAIR), 1) < HEAD_DIM
        row = lax.broadcasted_iota(jnp.int32, (2 * CONT, PROMPT), 0) % CONT
        past = lax.broadcasted_iota(jnp.int32, (2 * CONT, PROMPT), 1) - row
        own_ok = lax.broadcasted_iota(jnp.int32, (2 * CONT, CONT), 1) <= (
            lax.broadcasted_iota(jnp.int32, (2 * CONT, CONT), 0) % CONT
        )
        lane = lax.broadcasted_iota(jnp.int32, (2 * CONT, 128), 1)
        inverses = jnp.zeros((2 * CONT, 128), f32)
        zero = jnp.zeros((), b16)
        for pair in range(pairs):
            lanes = slice(pair * PAIR, (pair + 1) * PAIR)
            kp, vp = k[:PROMPT, lanes], v[:PROMPT, lanes]
            for sub in range(subs):
                unit = pair * subs + sub
                own = slice(PROMPT + sub * CONT, PROMPT + (sub + 1) * CONT)
                q2 = q[sub * CONT : (sub + 1) * CONT, lanes]
                qs = jnp.concatenate([jnp.where(low, q2, zero), jnp.where(low, zero, q2)], 0)
                first = t * rows + sub * CONT
                s1 = jnp.where(past <= first, dot(qs, kp, NT), MASKED)
                s2 = jnp.where(own_ok & (first >= PROMPT), dot(qs, k[own, lanes], NT), MASKED)
                top = jnp.maximum(jnp.max(s1, -1, keepdims=True), jnp.max(s2, -1, keepdims=True))
                e1 = jnp.exp(s1 - top)
                e2 = jnp.exp(s2 - top)
                inv = 1.0 / (jnp.sum(e1, -1, keepdims=True) + jnp.sum(e2, -1, keepdims=True))
                inverses = jnp.where(lane == unit, inv, inverses)
                p1 = e1.astype(b16)
                p2 = e2.astype(b16)
                at_p = slice(unit * 2 * CONT, (unit + 1) * 2 * CONT)
                p_ref[0, at_p, :PROMPT] = p1
                p_ref[0, at_p, PROMPT:] = p2
                c2 = (dot(p1, vp, NN) + dot(p2, v[own, lanes], NN)) * inv
                c_ref[sub * CONT : (sub + 1) * CONT, lanes] = jnp.where(low, c2[:CONT], c2[CONT:]).astype(b16)
        inv_ref[0] = inverses
        acc[...] += dot(c_ref[...], w_ref[0, 3], NT)

        @pl.when(step == groups - 1)
        def _():
            h = acc[...]
            h_ref[...] = h
            b_ref[...] = (unit_of(h)[0] * gain_ref[1:2]).astype(b16)

    def by_group(i, at):
        return (0, i)

    return pl.pallas_call(
        body,
        grid_spec=pltpu.PrefetchScalarGridSpec(
            num_scalar_prefetch=1,
            grid=(groups,),
            in_specs=[pl.BlockSpec((rows, width), whole)] * 4
            + [
                pl.BlockSpec(gains.shape, whole),
                pl.BlockSpec((1, 4, width, cols), lambda i, at: (i, 0, 0, 0)),
            ],
            out_specs=[
                pl.BlockSpec((tall, width), whole),
                pl.BlockSpec((rows, cols), by_group),
                pl.BlockSpec((tall, cols), by_group),
                pl.BlockSpec((tall, cols), by_group),
                pl.BlockSpec((1, 2 * pairs * rows, keys), lambda i, at: (i, 0, 0)),
                pl.BlockSpec((1, 2 * CONT, 128), lambda i, at: (i, 0, 0)),
                pl.BlockSpec((rows, cols), by_group),
                pl.BlockSpec((rows, width), whole),
                pl.BlockSpec((rows, width), whole),
            ],
            scratch_shapes=[pltpu.VMEM((4 * rows, width), b16), pltpu.VMEM((rows, width), f32)],
        ),
        out_shape=[
            jax.ShapeDtypeStruct((tall, width), b16),
            jax.ShapeDtypeStruct((rows, width), b16),
            jax.ShapeDtypeStruct((tall, width), b16),
            jax.ShapeDtypeStruct((tall, width), b16),
            jax.ShapeDtypeStruct((groups, 2 * pairs * rows, keys), b16),
            jax.ShapeDtypeStruct((groups, 2 * CONT, 128), f32),
            jax.ShapeDtypeStruct((rows, width), b16),
            jax.ShapeDtypeStruct((rows, width), f32),
            jax.ShapeDtypeStruct((rows, width), b16),
        ],
        compiler_params=params(56),
        cost_estimate=pl.CostEstimate(
            flops=(2 * width * width * (2 * tall + 2 * rows) + 8 * rows * keys * width) // ESTIMATE,
            bytes_accessed=60 * MIB // ESTIMATE,
            transcendentals=rows * keys * 16,
        ),
    )(at, *slots, gains, weights)


def attention_backward(base, count, given, gains, a, q, k, v, p, inv, c, weights, parts):
    opens = base == 0
    rows, width = q.shape
    _, _, _, cols = weights.shape
    tall = PROMPT + rows
    padded = -(-PROMPT // rows) * rows
    subs = rows // CONT
    pairs = cols // PAIR
    keys = PROMPT + CONT
    cut = width // parts

    def body(*refs):
        n_given = 5 if opens else 2
        given_refs = refs[:n_given]
        gain_ref, a_ref, q_ref, k_ref, v_ref, p_ref, inv_ref, c_ref, w_ref = refs[n_given : n_given + 9]
        dw_ref, *outs = refs[n_given + 9 : n_given + 13]
        do, ds, dqs, *more = refs[n_given + 13 :]
        step = pl.program_id(0)
        acc = outs[0] if opens else more[0]
        sum_ref = outs[2]

        @pl.when(step == 0)
        def _():
            sum_ref[...] = jnp.zeros_like(sum_ref)
            if opens:
                h_ref, dy_ref, *part_refs = given_refs
                d0, d1, d2 = (r[...].astype(f32) for r in part_refs)
                dn = d0 + d1 + d2
                gain = gain_ref[1:2]
                unit, scale = unit_of(h_ref[...])
                along = dn * gain
                inner = jnp.mean(along * unit, -1, keepdims=True)
                dh = dy_ref[...].astype(f32) + scale * (along - unit * inner)
                outs[1][...] = dh
                do[...] = dh.astype(b16)
                sum_ref[1:2] = jnp.sum(dn * unit, 0, keepdims=True)
                acc[...] = jnp.zeros_like(acc)
            else:
                do[...] = given_refs[0][...].astype(b16)
                acc[...] = given_refs[1][...]

        low = lax.broadcasted_iota(jnp.int32, (CONT, PAIR), 1) < HEAD_DIM
        zero = jnp.zeros((), b16)

        def stacked(two):
            return jnp.concatenate([jnp.where(low, two, zero), jnp.where(low, zero, two)], 0)

        def weight_out(kind, left, right):
            value = dot(left, right, TN).astype(b16)
            for n in range(value.shape[0] // cols):
                piece = value[n * cols : (n + 1) * cols]
                if cut % 128 == 0:
                    for s in range(parts):
                        dw_ref[s, 0, kind + n] = piece[:, s * cut : (s + 1) * cut]
                else:
                    dw_ref[0, 0, kind + n] = piece

        dc = dot(do[...], w_ref[0, 3], NN).astype(b16)
        weight_out(3, c_ref[...], do[...])
        dks, dvs = [], []
        for pair in range(pairs):
            lanes = slice(pair * PAIR, (pair + 1) * PAIR)
            kp, vp = k_ref[:PROMPT, lanes], v_ref[:PROMPT, lanes]
            qall, dcall, dko, dvo = [], [], [], []
            for sub in range(subs):
                n = pair * subs + sub
                own = slice(PROMPT + sub * CONT, PROMPT + (sub + 1) * CONT)
                mine = slice(sub * CONT, (sub + 1) * CONT)
                at_p = slice(n * 2 * CONT, (n + 1) * 2 * CONT)
                dcs = (stacked(dc[mine, lanes]).astype(f32) * inv_ref[0][:, n : n + 1]).astype(b16)
                qs = stacked(q_ref[mine, lanes])
                cs = stacked(c_ref[mine, lanes])
                delta = jnp.sum(dcs.astype(f32) * cs.astype(f32), -1, keepdims=True)
                p1 = p_ref[0, at_p, :PROMPT]
                p2 = p_ref[0, at_p, PROMPT:]
                ds1 = (p1.astype(f32) * (dot(dcs, vp, NT) - delta)).astype(b16)
                ds2 = (p2.astype(f32) * (dot(dcs, v_ref[own, lanes], NT) - delta)).astype(b16)
                ds[sub * 2 * CONT : (sub + 1) * 2 * CONT] = ds1
                dq2 = (dot(ds1, kp, NN) + dot(ds2, k_ref[own, lanes], NN)) * 0.125
                dqs[mine, lanes] = jnp.where(low, dq2[:CONT], dq2[CONT:]).astype(b16)
                dko.append(dot(ds2, qs, TN).astype(b16))
                dvo.append(dot(p2, dcs, TN).astype(b16))
                qall.append(qs)
                dcall.append(dcs)
            span = slice(pair * 2 * rows, (pair + 1) * 2 * rows)
            dkp = dot(ds[...], jnp.concatenate(qall, 0), TN).astype(b16)
            dvp = dot(p_ref[0, span, :PROMPT], jnp.concatenate(dcall, 0), TN).astype(b16)
            dks.append(jnp.concatenate([dkp] + dko, 0))
            dvs.append(jnp.concatenate([dvp] + dvo, 0))
        dkv = jnp.concatenate(dks + dvs, 1)
        dq = dqs[...]
        weight_out(0, dq, a_ref[PROMPT:tall])
        weight_out(1, dkv, a_ref[...])
        acc[...] += dot(dkv, jnp.concatenate([w_ref[0, 1], w_ref[0, 2]], 1), NT)
        acc[PROMPT:] += dot(dq, w_ref[0, 0], NT)

        if not opens:
            @pl.when(step == count - 1)
            def _():
                dap_ref, dao_ref = outs[:2]
                dap_ref[:PROMPT] = acc[:PROMPT].astype(b16)
                if padded > PROMPT:
                    dap_ref[PROMPT:] = jnp.zeros((padded - PROMPT, width), b16)
                dao_ref[...] = acc[PROMPT:]
                total = jnp.sum(acc[...] * a_ref[...].astype(f32), 0, keepdims=True)
                sum_ref[0:1] = total / gain_ref[0:1]

    def by_group(i):
        return (0, base + i)

    row_spec = pl.BlockSpec((rows, width), whole)
    tall_spec = pl.BlockSpec((tall, width), whole)
    places, lanes_out = (parts, cut) if cut % 128 == 0 else (1, width)
    if opens:
        first_out, first_shape = tall_spec, jax.ShapeDtypeStruct((tall, width), f32)
    else:
        first_out, first_shape = pl.BlockSpec((padded, width), whole), jax.ShapeDtypeStruct((padded, width), b16)
    return pl.pallas_call(
        body,
        grid=(count,),
        in_specs=([row_spec] * 5 if opens else [row_spec, tall_spec])
        + [
            pl.BlockSpec(gains.shape, whole),
            tall_spec,
            pl.BlockSpec((rows, cols), by_group),
            pl.BlockSpec((tall, cols), by_group),
            pl.BlockSpec((tall, cols), by_group),
            pl.BlockSpec((1, 2 * pairs * rows, keys), lambda i: (base + i, 0, 0)),
            pl.BlockSpec((1, 2 * CONT, 128), lambda i: (base + i, 0, 0)),
            pl.BlockSpec((rows, cols), by_group),
            pl.BlockSpec((1, 4, width, cols), lambda i: (base + i, 0, 0, 0)),
        ],
        out_specs=[
            pl.BlockSpec((places, 1, 4, cols, lanes_out), lambda i: (0, i, 0, 0, 0)),
            first_out,
            row_spec,
            pl.BlockSpec((8, width), whole),
        ],
        scratch_shapes=[
            pltpu.VMEM((rows, width), b16),
            pltpu.VMEM((2 * rows, PROMPT), b16),
            pltpu.VMEM((rows, cols), b16),
        ]
        + ([] if opens else [pltpu.VMEM((tall, width), f32)]),
        out_shape=[
            jax.ShapeDtypeStruct((places, count, 4, cols, lanes_out), b16),
            first_shape,
            jax.ShapeDtypeStruct((rows, width), f32),
            jax.ShapeDtypeStruct((8, width), f32),
        ],
        compiler_params=params(60),
        cost_estimate=pl.CostEstimate(
            flops=count * (width * width * (2 * tall + 2 * rows) + 4 * rows * keys * width) // ESTIMATE,
            bytes_accessed=count * 20 * MIB // ESTIMATE,
            transcendentals=0,
        ),
    )(*given, gains, a, q, k, v, p, inv, c, weights)


def experts_blocks(blocks, given, keep, router, weights, start, own, experts, ends):
    rows, width = given[0].shape
    if not ends:
        rows = 2 * rows
    one = rows // 2
    units = weights.shape[1]
    n_given = len(given)

    def body(blocks_ref, *refs):
        given_refs = refs[:n_given]
        keep_a, keep_b, r_ref, wg_ref, wu_ref, wd_ref = refs[n_given : n_given + 6]
        refs = refs[n_given + 6 :]
        if ends:
            b_ref, dy_ref, y_in, db_in, dgates_in = given_refs
            y0, y1, db0, db1, rg_ref, z_ref, dg_ref, du_ref = refs
        else:
            b_ref, dy_ref, y_acc, db_acc, dgates_ref, z_ref, dg_ref, du_ref = refs
        lane = lax.broadcasted_iota(jnp.int32, (one, 128), 1)
        col = lax.broadcasted_iota(jnp.int32, (one, units), 1)
        met = range(start // own, (start + units - 1) // own + 1)
        for n in range(2):
            span = slice(n * one, (n + 1) * one)
            keep = (keep_a, keep_b)[n][...]
            if ends:
                b_v, dy_v = b_ref[span], dy_ref[span]
            else:
                b_v, dy_v = given_refs[n][...], given_refs[2 + n][...]
                b_ref[span] = b_v
                dy_ref[span] = dy_v
            logits = dot(b_v, r_ref[...], NN)
            live = lane < experts
            top = jnp.max(jnp.where(live, logits, MASKED), -1, keepdims=True)
            grown = jnp.exp(jnp.where(lane < 2 * experts, logits, MASKED) - top)
            share = grown / jnp.sum(jnp.where(live, grown, 0.0), -1, keepdims=True)
            gates = share.astype(b16).astype(f32) * keep

            g = dot(b_v, wg_ref[0], NT)
            u = dot(b_v, wu_ref[0], NT)
            dz_plain = dot(dy_v, wd_ref[0], NT)
            gate = gates[:, met[-1] : met[-1] + 1]
            for expert in met[-2::-1]:
                gate = jnp.where(col < (expert + 1) * own - start, gates[:, expert : expert + 1], gate)
            cdf, pdf = normal(g)
            act = g * cdf
            z = (act * u).astype(b16).astype(f32)
            along = dz_plain * z
            dgates = dgates_in[span] if ends else jnp.zeros((one, 128), f32)
            for expert in met:
                low, high = max(expert * own - start, 0), min((expert + 1) * own - start, units)
                inner_low, inner_high = -(-low // 128) * 128, high // 128 * 128
                part = jnp.sum(along[:, inner_low:inner_high], -1, keepdims=True)
                if low < inner_low:
                    edge = along[:, inner_low - 128 : inner_low]
                    part += jnp.sum(jnp.where(lane >= low % 128, edge, 0.0), -1, keepdims=True)
                if inner_high < high:
                    edge = along[:, inner_high : inner_high + 128]
                    part += jnp.sum(jnp.where(lane < high % 128, edge, 0.0), -1, keepdims=True)
                dgates += jnp.where(lane % experts == expert, part, 0.0)
            dz = dz_plain * gate
            dg = (dz * u * (cdf + g * pdf)).astype(b16)
            du = (dz * act).astype(b16)
            zg = (z * gate).astype(b16)
            z_ref[span] = zg
            dg_ref[span] = dg
            du_ref[span] = du
            y = dot(zg, wd_ref[0], NN)
            db = dot(dg, wg_ref[0], NN) + dot(du, wu_ref[0], NN)
            if not ends:
                y_acc[span] = y
                db_acc[span] = db
                dgates_ref[span] = dgates
            else:
                dprob = dgates * keep
                inner = jnp.sum(jnp.where(lane < experts, share * dprob, 0.0), -1, keepdims=True)
                dl = jnp.where(lane < 2 * experts, share * (dprob - inner), 0.0)
                head = dl.astype(b16).astype(f32)
                split = jnp.where(lane < experts, head, dl - head).astype(b16)
                if n == 0:
                    rg_ref[...] = dot(b_v, split, TN)
                else:
                    rg_ref[...] += dot(b_v, split, TN)
                (y0, y1)[n][...] = (y + y_in[span]).astype(b16)
                (db0, db1)[n][...] = (db + db_in[span] + dot(split, r_ref[...], NT)).astype(b16)

    def weight(kind):
        return pl.BlockSpec((1, units, width), lambda i, at: (kind, 0, 0))

    hidden = pl.BlockSpec((rows, units), whole)
    one_spec = pl.BlockSpec((one, width), whole)
    both_spec = pl.BlockSpec((rows, width), whole)
    gate_spec = pl.BlockSpec((rows, 128), whole)
    both = jax.ShapeDtypeStruct((rows, width), b16)
    sums = jax.ShapeDtypeStruct((rows, width), f32)
    if ends:
        outs = [(one_spec, jax.ShapeDtypeStruct((one, width), b16))] * 4
        outs += [(pl.BlockSpec((width, 128), whole), jax.ShapeDtypeStruct((width, 128), f32))]
    else:
        outs = [(both_spec, both)] * 2 + [(both_spec, sums)] * 2
        outs += [(gate_spec, jax.ShapeDtypeStruct((rows, 128), f32))]
    outs += [(hidden, jax.ShapeDtypeStruct((rows, units), b16))] * 3
    return pl.pallas_call(
        body,
        grid_spec=pltpu.PrefetchScalarGridSpec(
            num_scalar_prefetch=1,
            grid=(1,),
            in_specs=([both_spec] * 4 + [gate_spec] if ends else [one_spec] * 4)
            + [
                pl.BlockSpec((one, 128), lambda i, at: (at[0], 0)),
                pl.BlockSpec((one, 128), lambda i, at: (at[1], 0)),
                pl.BlockSpec((width, 128), whole),
                weight(0),
                weight(1),
                weight(2),
            ],
            out_specs=[spec for spec, _ in outs],
        ),
        out_shape=[shape for _, shape in outs],
        compiler_params=params(60),
        cost_estimate=pl.CostEstimate(
            flops=(12 * rows * width * units) // ESTIMATE,
            bytes_accessed=(6 * units * width + 6 * rows * units) // ESTIMATE,
            transcendentals=2 * rows * units,
        ),
    )(blocks, *given, keep, keep, router, weights, weights, weights)


def experts_weights(me, bs, dys, opened, closed, parts):
    pieces = len(bs)
    rows, width = bs[0].shape
    first_units, last_units = opened[0][0].shape[1], closed[0][0].shape[1]
    units = first_units + last_units
    chunk = UNIT_CHUNK
    turn = first_units // chunk
    cut = width // parts
    blocked = cut % 128 == 0

    def body(me_ref, *refs):
        b_refs, dy_refs = refs[:pieces], refs[pieces : 2 * pieces]
        begun = refs[2 * pieces : 5 * pieces]
        ended = refs[5 * pieces : 8 * pieces]
        near, far, held = refs[8 * pieces :]

        def run(hidden):
            for kind, right in enumerate((b_refs, b_refs, dy_refs)):
                left = [hidden[n * 3 + (kind + 1) % 3] for n in range(pieces)]
                value = dot(left[0][...], right[0][...], TN)
                for n in range(1, pieces):
                    value += dot(left[n][...], right[n][...], TN)
                held[kind] = value.astype(b16)

        @pl.when(pl.program_id(0) < turn)
        def _():
            run(begun)

        @pl.when(pl.program_id(0) >= turn)
        def _():
            run(ended)

        for kind in range(3):
            for s in range(parts if blocked else 0):
                lanes = pl.ds(pl.multiple_of((me_ref[0] ^ s) * cut, cut), cut)
                (far if s % 2 else near)[s // 2, kind] = held[kind, :, lanes]
            if not blocked:
                near[0, kind] = held[kind, :, : width // 2]
                far[0, kind] = held[kind, :, width // 2 :]

    places, lanes = (parts // 2, cut) if blocked else (1, width // 2)
    return pl.pallas_call(
        body,
        grid_spec=pltpu.PrefetchScalarGridSpec(
            num_scalar_prefetch=1,
            grid=(units // chunk,),
            in_specs=[pl.BlockSpec((rows, width), whole)] * (2 * pieces)
            + [pl.BlockSpec((rows, chunk), lambda i, me: (0, jnp.minimum(i, turn - 1)))] * (3 * pieces)
            + [pl.BlockSpec((rows, chunk), lambda i, me: (0, jnp.maximum(i - turn, 0)))] * (3 * pieces),
            out_specs=[pl.BlockSpec((places, 3, chunk, lanes), lambda i, me: (0, 0, i, 0))] * 2,
            scratch_shapes=[pltpu.VMEM((3, chunk, width), b16)],
        ),
        out_shape=[jax.ShapeDtypeStruct((places, 3, units, lanes), b16)] * 2,
        compiler_params=params(56),
        cost_estimate=pl.CostEstimate(
            flops=6 * pieces * rows * width * units // ESTIMATE,
            bytes_accessed=(6 * units * width + 6 * pieces * rows * units) // ESTIMATE,
            transcendentals=0,
        ),
    )(me, *bs, *dys, *(v for part in opened for v in part), *(v for part in closed for v in part))


class Halving:
    def __init__(self, near, other, low, high):
        places = near.shape[0]
        half = (high - low) // 2
        bits = [1 << n for n in range(places.bit_length() - 1)]
        self.orders = [bits, bits[::-1]]
        self.held = []
        for path in range(2):
            span = slice(low + path * half, low + (path + 1) * half)
            self.held.append({s: near[s, span].astype(f32) + other[s, span].astype(f32) for s in range(places)})

    def sends(self):
        self.bits = [order.pop(0) for order in self.orders]
        out = []
        for held, bit in zip(self.held, self.bits):
            out.append((jnp.concatenate([held[s] for s in held if s & bit], 0).astype(b16), 2 * bit, "dp"))
        return out

    def take(self, got):
        for path, (held, bit, came) in enumerate(zip(self.held, self.bits, got)):
            away = [s for s in held if s & bit]
            size = came.shape[0] // len(away)
            self.held[path] = {s ^ bit: held[s ^ bit] + came[n * size : (n + 1) * size].astype(f32) for n, s in enumerate(away)}

    def result(self):
        return jnp.concatenate([held[0] for held in self.held], 0)


def input_gradient(dh, own, piece, sent, x, gains):
    rows, width = dh.shape

    def body(dh_ref, own_ref, piece_ref, sent_ref, x_ref, gain_ref, out_ref):
        da = own_ref[...] + (piece_ref[...].astype(f32) + sent_ref[...].astype(f32))
        unit, scale = unit_of(x_ref[...].astype(f32))
        along = da * gain_ref[0:1]
        inner = jnp.mean(along * unit, -1, keepdims=True)
        out_ref[...] = dh_ref[...] + scale * (along - unit * inner)

    block = pl.BlockSpec((CONT, width), lambda i: (i, 0))
    return pl.pallas_call(
        body,
        grid=(rows // CONT,),
        in_specs=[block] * 5 + [pl.BlockSpec(gains.shape, whole)],
        out_specs=block,
        out_shape=jax.ShapeDtypeStruct((rows, width), f32),
        compiler_params=params(32),
    )(dh, own, piece, sent, x, gains)


def on_device(inputs, cotangent, attn_gain, moe_gain, router, w_query, w_key, w_value, w_out, w_gate, w_up, w_down, expert_ids, priority):
    rows, width = inputs.shape
    experts, cut, own_units = w_gate.shape
    units = experts * own_units
    dp = lax.axis_size("dp")
    depth = lax.axis_size("tensor")
    own = lax.axis_index("tensor")
    me = lax.axis_index("dp")
    at = jnp.full((1,), own, jnp.int32)
    here = jnp.full((1,), me, jnp.int32)
    up = [(i, i + 1) for i in range(depth - 1)]
    down = [(i + 1, i) for i in range(depth - 1)]
    together = lax.optimization_barrier

    def swap(value, bits, axis="tensor"):
        size = depth if axis == "tensor" else dp
        return lax.ppermute(value, axis, [(i, i ^ bits) for i in range(size)])

    def raised(value):
        return lax.ppermute(value, "tensor", up)

    mine = jnp.stack([w_query, w_key, w_value, w_out.T])
    far = swap(mine, 2)
    attention_w = jnp.stack([mine, swap(mine, 1), far, swap(far, 1)])
    attention_w = lax.all_gather(attention_w, "dp", axis=2, tiled=True)

    small = jnp.concatenate([attn_gain[None], moe_gain[None], router.T, jnp.zeros((2, router.shape[0]), b16)], 0)

    def doubled(small, other, index, bit):
        return jnp.where(index & bit != 0, jnp.concatenate([other, small], 1), jnp.concatenate([small, other], 1))

    for bit in [1 << n for n in range(dp.bit_length() - 1)]:
        small = doubled(small, swap(small, bit, "dp"), me, bit)
    x1, other = together((raised(inputs), swap(small, 1)))
    small = doubled(small, other, own, 1)
    x2, other = together((raised(x1), swap(small, 2)))
    small = doubled(small, other, own, 2)
    small = small.reshape(8, depth, dp, -1).swapaxes(1, 2).reshape(8, width)
    x3 = raised(x2)
    gains = small.astype(f32)
    router_full = small[2 : 2 + experts].T
    router_wide = jnp.concatenate(
        [router_full, router_full, jnp.zeros((width, 128 - 2 * experts), b16)], 1
    )
    keep = keep_mask(expert_ids.T, priority.reshape(-1, 2).T, experts)

    shards = [w_gate.transpose(0, 2, 1), w_up.transpose(0, 2, 1), w_down]
    shards = jnp.stack([shard.reshape(units, cut) for shard in shards])
    middle = FIRST_CHUNKS * UNIT_CHUNK
    halves = [
        lax.all_gather(piece, "dp", axis=2, tiled=True)
        for piece in (shards[:, :middle], shards[:, middle:])
    ]

    x3, gains, dy0, keep, router_wide = together((x3, gains, cotangent, keep, router_wide))
    dy1, dy2 = swap(dy0, 1), swap(dy0, 2)
    a, q, k, v, p, inv, c, h, b = attention_forward(at, (inputs, x1, x2, x3), gains, attention_w)
    b, dy1, dy2 = together((b, dy1, dy2))
    b2 = swap(b, 2)
    bs = (b, swap(b, 1), b2, swap(b2, 1))
    dys = (dy0, dy1, dy2, swap(dy2, 1))

    def run(pair, half, given):
        blocks = jnp.stack([own ^ (2 * pair), own ^ (2 * pair + 1)]).astype(jnp.int32)
        return experts_blocks(blocks, given, keep, router_wide, halves[half], half * middle, own_units, experts, half == 1)

    opened_0 = run(0, 0, (bs[0], bs[1], dys[0], dys[1]))
    second, opened_0 = together(((bs[2], bs[3], dys[2], dys[3]), opened_0))
    opened_1 = run(1, 0, second)
    closed_1 = run(1, 1, opened_1[:5])
    opened_0, closed_1 = together((opened_0, closed_1))
    near3 = swap(closed_1[3], 1)
    closed_0 = run(0, 1, opened_0[:5])
    closed_0, near3 = together((closed_0, near3))
    joined = [opened_0[0], opened_1[0]], [opened_0[1], opened_1[1]]
    d1, d2 = closed_0[3], closed_1[2] + near3
    d1, d2, joined = together((d1, d2, joined))
    near, far = experts_weights(here, *joined, (opened_0[5:], opened_1[5:]), (closed_0[5:], closed_1[5:]), dp)
    d1, d2, near, far = together((swap(d1, 1), swap(d2, 2), near, far))
    blocked = cut % 128 == 0

    def stage(sends, given=(), work=None):
        values, given = together((tuple(value for value, *_ in sends), given))
        got = tuple(swap(value, *how) if how else lax.ppermute(value, "tensor", down) for value, (_, *how) in zip(values, sends))
        return together((got, work(given) if work else given))

    def backward(base):
        return lambda given: attention_backward(base, 2, given, gains, a, q, k, v, p, inv, c, attention_w, dp)

    def summed(dw):
        if blocked:
            return lax.psum_scatter(dw, "dp", scatter_dimension=0, tiled=True)[0]
        return lax.psum_scatter(dw[0], "dp", scatter_dimension=3, tiled=True)

    sends = [(far, 1, "dp")] if blocked else []
    given = (h, cotangent, closed_0[2], d1, d2)
    got, opened = stage(sends + [(closed_1[1], 1)], given, backward(0))
    heads_0 = summed(opened[0])
    y2 = closed_1[0] + got[-1]
    halvings = []
    if blocked:
        lines = 3 * units
        near = near.reshape(dp // 2, lines, cut)
        other = got[0].reshape(dp // 2, lines, cut)
        halvings = [Halving(near, other, 0, lines // 2), Halving(near, other, lines // 2, lines)]
    sends = halvings[0].sends() if blocked else []
    got, closed = stage(sends + [(closed_0[1], 1), (y2, 2)], (opened[2], opened[1]), backward(2))
    y1, y2 = got[-2:]
    if blocked:
        halvings[0].take(got[:2])
    heads_1 = summed(closed[0])
    dap, dao, dh = closed[1], closed[2], opened[2]

    def chunk_of(index):
        start = jnp.clip(index, 0, dap.shape[0] // rows - 1) * rows
        piece = lax.dynamic_slice_in_dim(dap, start, rows, 0)
        valid = (index >= 0) & (index < dap.shape[0] // rows)
        return jnp.where(valid, piece, jnp.zeros((), b16))

    rg = closed_0[4] + closed_1[4]
    rg = (rg[:, :experts] + rg[:, experts : 2 * experts]).T
    small_grad = jnp.concatenate([opened[3][:2] + closed[3][:2], rg], 0)
    sends = halvings[1].sends() if blocked else []
    got, small_grad = stage([(chunk_of(own - depth + 1),)] + sends, small_grad, lambda v: lax.psum(v, "tensor"))
    sent = got[0]
    if blocked:
        halvings[1].take(got[1:])
    pairs = [halving.sends() for halving in halvings if halving.orders[0]]
    sends = [(jnp.concatenate([one[0], two[0]], 0), *one[1:]) for one, two in zip(*pairs)] if pairs else []
    got, small_grad = stage([(chunk_of(own - depth + 2) + sent,)] + sends, small_grad, lambda v: lax.psum(v, "dp"))
    sent = got[0]
    if sends:
        for n, halving in enumerate(halvings):
            halving.take([came[n * came.shape[0] // 2 : (n + 1) * came.shape[0] // 2] for came in got[1:]])
    sent = lax.ppermute(chunk_of(own - depth + 3) + sent, "tensor", down)
    for halving in halvings:
        while halving.orders[0]:
            halving.take([swap(*send) for send in halving.sends()])

    slots = jnp.concatenate([heads_0, heads_1], 0)
    total = slots[0].astype(f32)
    for s in range(1, depth):
        total = total + swap(slots[s], s).astype(f32)
    count = width // (dp * depth)
    small_grad = lax.dynamic_slice_in_dim(small_grad, (me * depth + own) * count, count, 1)
    input_grad = input_gradient(dh, dao, chunk_of(own), sent, inputs, gains)
    output = h + closed_0[0].astype(f32) + y1.astype(f32) + y2.astype(f32)

    if blocked:
        total_units = jnp.concatenate([halving.result() for halving in halvings], 0).reshape(3, units, cut)
    else:
        pieces = jnp.concatenate([near[0], far[0]], -1)
        total_units = lax.psum_scatter(pieces, "dp", scatter_dimension=2, tiled=True).astype(f32)
    wg_grad, wu_grad, wd_grad = (total_units[n].reshape(experts, own_units, cut) for n in range(3))
    return (
        output.astype(b16),
        input_grad,
        small_grad[0],
        small_grad[1],
        small_grad[2:].T,
        total[0].T,
        total[1].T,
        total[2].T,
        total[3],
        wg_grad.transpose(0, 2, 1),
        wu_grad.transpose(0, 2, 1),
        wd_grad,
    )


def solution(mesh):
    tokens = P(("dp", "tensor"), None)
    vector = P(("dp", "tensor"))
    return jax.shard_map(
        on_device,
        mesh=mesh,
        in_specs=(tokens, tokens, vector, vector, tokens)
        + (P("dp", "tensor"),) * 3
        + (P("tensor", "dp"), P(None, "dp", "tensor"), P(None, "dp", "tensor"), P(None, "tensor", "dp"))
        + (P("dp", None), P("dp", None)),
        out_specs=(tokens, tokens, vector, vector, tokens)
        + (P("dp", "tensor"),) * 3
        + (P("tensor", "dp"), P(None, "dp", "tensor"), P(None, "dp", "tensor"), P(None, "tensor", "dp")),
        check_vma=False,
    )
```

```python
import jax
import jax.numpy as jnp
from jax import lax
from jax.experimental import pallas as pl
from jax.experimental.pallas import tpu as pltpu
from jax.sharding import PartitionSpec as P

HEAD_DIM = 64
PROMPT = 1024
CONT = 128
CAPACITY = 960
EPS = 1e-06
PAIR = 2 * HEAD_DIM
MIB = 2**20

f32 = jnp.float32
b16 = jnp.bfloat16
NN = (((1,), (0,)), ((), ()))
NT = (((1,), (1,)), ((), ()))
TN = (((0,), (0,)), ((), ()))
INV_SQRT2 = 0.7071067811865476
INV_SQRT_2PI = 0.3989422804014327
MASKED = -1e30
SMALL_ROWS = 32
UNIT_CHUNK = 256
ESTIMATE = 4
FIRST_CHUNKS = 6


def dot(left, right, dims):
    return lax.dot_general(left, right, dims, preferred_element_type=f32)


def params(mib):
    return pltpu.CompilerParams(vmem_limit_bytes=mib * MIB)


def whole(*_):
    return (0, 0)


def unit_of(values):
    scale = lax.rsqrt(jnp.mean(values * values, -1, keepdims=True) + EPS)
    return values * scale, scale


def normal(v):
    bell = jnp.exp(-0.5 * v * v)
    t = 1.0 / (1.0 + (0.3275911 * INV_SQRT2) * jnp.abs(v))
    poly = t * (0.127414796 + t * (-0.142248368 + t * (0.710706871 + t * (-0.726576014 + t * 0.530702715))))
    tail = poly * bell
    return jnp.where(v < 0.0, tail, 1.0 - tail), INV_SQRT_2PI * bell


def keep_mask(ids, order, experts):
    rows = ids.shape[1]
    pairs = ids.shape[0] * rows
    bits = pairs.bit_length()

    def body(ids_ref, order_ref, keep_ref):
        ids_v = ids_ref[...]
        order_v = order_ref[...]
        sub = lax.broadcasted_iota(jnp.int32, (128, rows), 0)
        out = jnp.zeros((128, rows), f32)
        for expert in range(experts):
            mine = ids_v == expert
            bound = jnp.zeros((1, 1), jnp.int32)
            for bit in range(bits - 1, -1, -1):
                trial = bound + (1 << bit)
                inside = jnp.where(mine & (order_v < trial), 1.0, 0.0)
                count = jnp.sum(jnp.sum(inside, 1, keepdims=True), 0, keepdims=True)
                bound = jnp.where(count <= CAPACITY, trial, bound)
            kept = jnp.sum(jnp.where(mine & (order_v < bound), 1.0, 0.0), 0, keepdims=True)
            out = jnp.where((sub < 2 * experts) & (sub % experts == expert), kept, out)
        keep_ref[...] = jnp.transpose(out)

    return pl.pallas_call(
        body,
        out_shape=jax.ShapeDtypeStruct((rows, 128), f32),
        compiler_params=params(32),
    )(ids, order)


def attention_forward(at, slots, gains, weights):
    rows, width = slots[0].shape
    groups, _, _, cols = weights.shape
    tall = PROMPT + rows
    subs = rows // CONT
    pairs = cols // PAIR
    keys = PROMPT + CONT

    def body(at_ref, x0, x1, x2, x3, gain_ref, w_ref, a_ref, q_ref, k_ref, v_ref, p_ref, inv_ref, c_ref, h_ref, b_ref, xs, acc):
        step = pl.program_id(0)
        t = at_ref[0]

        @pl.when(step == 0)
        def _():
            for s, x in enumerate((x0, x1, x2, x3)):
                xs[s * rows : (s + 1) * rows] = x[...]
            gain = gain_ref[0:1]
            for start in range(0, PROMPT, rows):
                take = min(rows, PROMPT - start)
                slot = jnp.maximum(t - start // rows, 0)
                x = xs[pl.ds(pl.multiple_of(slot * rows, 128), take)].astype(f32)
                a_ref[start : start + take] = (unit_of(x)[0] * gain).astype(b16)
            x = x0[...].astype(f32)
            a_ref[PROMPT:tall] = (unit_of(x)[0] * gain).astype(b16)
            acc[...] = x

        q = dot(a_ref[PROMPT:tall], w_ref[0, 0], NN).astype(b16) * jnp.asarray(0.125, b16)
        kv = dot(a_ref[...], jnp.concatenate([w_ref[0, 1], w_ref[0, 2]], 1), NN).astype(b16)
        k, v = kv[:, :cols], kv[:, cols:]
        q_ref[...] = q
        k_ref[...] = k
        v_ref[...] = v
        low = lax.broadcasted_iota(jnp.int32, (CONT, PAIR), 1) < HEAD_DIM
        row = lax.broadcasted_iota(jnp.int32, (2 * CONT, PROMPT), 0) % CONT
        past = lax.broadcasted_iota(jnp.int32, (2 * CONT, PROMPT), 1) - row
        own_ok = lax.broadcasted_iota(jnp.int32, (2 * CONT, CONT), 1) <= (
            lax.broadcasted_iota(jnp.int32, (2 * CONT, CONT), 0) % CONT
        )
        lane = lax.broadcasted_iota(jnp.int32, (2 * CONT, 128), 1)
        inverses = jnp.zeros((2 * CONT, 128), f32)
        zero = jnp.zeros((), b16)
        for pair in range(pairs):
            lanes = slice(pair * PAIR, (pair + 1) * PAIR)
            kp, vp = k[:PROMPT, lanes], v[:PROMPT, lanes]
            for sub in range(subs):
                unit = pair * subs + sub
                own = slice(PROMPT + sub * CONT, PROMPT + (sub + 1) * CONT)
                q2 = q[sub * CONT : (sub + 1) * CONT, lanes]
                qs = jnp.concatenate([jnp.where(low, q2, zero), jnp.where(low, zero, q2)], 0)
                first = t * rows + sub * CONT
                s1 = jnp.where(past <= first, dot(qs, kp, NT), MASKED)
                s2 = jnp.where(own_ok & (first >= PROMPT), dot(qs, k[own, lanes], NT), MASKED)
                top = jnp.maximum(jnp.max(s1, -1, keepdims=True), jnp.max(s2, -1, keepdims=True))
                e1 = jnp.exp(s1 - top)
                e2 = jnp.exp(s2 - top)
                inv = 1.0 / (jnp.sum(e1, -1, keepdims=True) + jnp.sum(e2, -1, keepdims=True))
                inverses = jnp.where(lane == unit, inv, inverses)
                p1 = e1.astype(b16)
                p2 = e2.astype(b16)
                at_p = slice(unit * 2 * CONT, (unit + 1) * 2 * CONT)
                p_ref[0, at_p, :PROMPT] = p1
                p_ref[0, at_p, PROMPT:] = p2
                c2 = (dot(p1, vp, NN) + dot(p2, v[own, lanes], NN)) * inv
                c_ref[sub * CONT : (sub + 1) * CONT, lanes] = jnp.where(low, c2[:CONT], c2[CONT:]).astype(b16)
        inv_ref[0] = inverses
        acc[...] += dot(c_ref[...], w_ref[0, 3], NT)

        @pl.when(step == groups - 1)
        def _():
            h = acc[...]
            h_ref[...] = h
            b_ref[...] = (unit_of(h)[0] * gain_ref[1:2]).astype(b16)

    def by_group(i, at):
        return (0, i)

    return pl.pallas_call(
        body,
        grid_spec=pltpu.PrefetchScalarGridSpec(
            num_scalar_prefetch=1,
            grid=(groups,),
            in_specs=[pl.BlockSpec((rows, width), whole)] * 4
            + [
                pl.BlockSpec(gains.shape, whole),
                pl.BlockSpec((1, 4, width, cols), lambda i, at: (i, 0, 0, 0)),
            ],
            out_specs=[
                pl.BlockSpec((tall, width), whole),
                pl.BlockSpec((rows, cols), by_group),
                pl.BlockSpec((tall, cols), by_group),
                pl.BlockSpec((tall, cols), by_group),
                pl.BlockSpec((1, 2 * pairs * rows, keys), lambda i, at: (i, 0, 0)),
                pl.BlockSpec((1, 2 * CONT, 128), lambda i, at: (i, 0, 0)),
                pl.BlockSpec((rows, cols), by_group),
                pl.BlockSpec((rows, width), whole),
                pl.BlockSpec((rows, width), whole),
            ],
            scratch_shapes=[pltpu.VMEM((4 * rows, width), b16), pltpu.VMEM((rows, width), f32)],
        ),
        out_shape=[
            jax.ShapeDtypeStruct((tall, width), b16),
            jax.ShapeDtypeStruct((rows, width), b16),
            jax.ShapeDtypeStruct((tall, width), b16),
            jax.ShapeDtypeStruct((tall, width), b16),
            jax.ShapeDtypeStruct((groups, 2 * pairs * rows, keys), b16),
            jax.ShapeDtypeStruct((groups, 2 * CONT, 128), f32),
            jax.ShapeDtypeStruct((rows, width), b16),
            jax.ShapeDtypeStruct((rows, width), f32),
            jax.ShapeDtypeStruct((rows, width), b16),
        ],
        compiler_params=params(56),
        cost_estimate=pl.CostEstimate(
            flops=(2 * width * width * (2 * tall + 2 * rows) + 8 * rows * keys * width) // ESTIMATE,
            bytes_accessed=60 * MIB // ESTIMATE,
            transcendentals=rows * keys * 16,
        ),
    )(at, *slots, gains, weights)


def attention_backward(me, base, count, given, rest, gains, a, q, k, v, p, inv, c, weights, parts):
    opens = base == 0
    rows, width = q.shape
    _, _, _, cols = weights.shape
    tall = PROMPT + rows
    padded = -(-PROMPT // rows) * rows
    subs = rows // CONT
    pairs = cols // PAIR
    keys = PROMPT + CONT
    cut = width // parts
    blocked = cut % 128 == 0
    places, lanes_out = (parts // 2, cut) if blocked else (1, width // 2)

    def body(me_ref, *refs):
        n_given = 6 if opens else 2
        given_refs = refs[:n_given]
        gain_ref, a_ref, q_ref, k_ref, v_ref, p_ref, inv_ref, c_ref, w_ref = refs[n_given : n_given + 9]
        rest_refs = refs[n_given + 9 : n_given + 9 + len(rest)]
        refs = refs[n_given + 9 + len(rest) :]
        near, far, first_out, row_out, *refs = refs
        if opens:
            sum_ref, *refs = refs
        do, ds, dqs, held, *more = refs
        step = pl.program_id(0)
        acc = first_out if opens else more[0]

        @pl.when(step == 0)
        def _():
            if opens:
                h_ref, dy_ref, *part_refs = given_refs
                d0, d1 = (r[...].astype(f32) for r in part_refs[:2])
                dn = d0 + d1 + jnp.concatenate([r[...] for r in part_refs[2:]], 0).astype(f32)
                gain = gain_ref[1:2]
                unit, scale = unit_of(h_ref[...])
                along = dn * gain
                inner = jnp.mean(along * unit, -1, keepdims=True)
                dh = dy_ref[...].astype(f32) + scale * (along - unit * inner)
                row_out[...] = dh
                do[...] = dh.astype(b16)
                sum_ref[...] = jnp.broadcast_to(jnp.sum(dn * unit, 0, keepdims=True), sum_ref.shape)
                acc[...] = jnp.zeros_like(acc)
            else:
                do[...] = given_refs[0][...].astype(b16)
                acc[...] = given_refs[1][...]

        low = lax.broadcasted_iota(jnp.int32, (CONT, PAIR), 1) < HEAD_DIM
        zero = jnp.zeros((), b16)

        def stacked(two):
            return jnp.concatenate([jnp.where(low, two, zero), jnp.where(low, zero, two)], 0)

        def cut_out(span, piece):
            count = piece.shape[0]
            held[:count] = piece
            for s in range(parts if blocked else 2):
                start = (me_ref[0] ^ s) * cut if blocked else s * lanes_out
                lanes = pl.ds(pl.multiple_of(start, lanes_out), lanes_out)
                (far if s % 2 else near)[s // 2, span] = held[:count, lanes]

        def weight_out(kind, left, right):
            value = dot(left, right, TN).astype(b16)
            for n in range(value.shape[0] // cols):
                piece = value[n * cols : (n + 1) * cols]
                cut_out(pl.ds(pl.multiple_of((step * 4 + kind + n) * cols, 128), cols), piece)

        dc = dot(do[...], w_ref[0, 3], NN).astype(b16)
        weight_out(3, c_ref[...], do[...])
        dks, dvs = [], []
        for pair in range(pairs):
            lanes = slice(pair * PAIR, (pair + 1) * PAIR)
            kp, vp = k_ref[:PROMPT, lanes], v_ref[:PROMPT, lanes]
            qall, dcall, dko, dvo = [], [], [], []
            for sub in range(subs):
                n = pair * subs + sub
                own = slice(PROMPT + sub * CONT, PROMPT + (sub + 1) * CONT)
                mine = slice(sub * CONT, (sub + 1) * CONT)
                at_p = slice(n * 2 * CONT, (n + 1) * 2 * CONT)
                dcs = (stacked(dc[mine, lanes]).astype(f32) * inv_ref[0][:, n : n + 1]).astype(b16)
                qs = stacked(q_ref[mine, lanes])
                cs = stacked(c_ref[mine, lanes])
                delta = jnp.sum(dcs.astype(f32) * cs.astype(f32), -1, keepdims=True)
                p1 = p_ref[0, at_p, :PROMPT]
                p2 = p_ref[0, at_p, PROMPT:]
                ds1 = (p1.astype(f32) * (dot(dcs, vp, NT) - delta)).astype(b16)
                ds2 = (p2.astype(f32) * (dot(dcs, v_ref[own, lanes], NT) - delta)).astype(b16)
                ds[sub * 2 * CONT : (sub + 1) * 2 * CONT] = ds1
                dq2 = (dot(ds1, kp, NN) + dot(ds2, k_ref[own, lanes], NN)) * 0.125
                dqs[mine, lanes] = jnp.where(low, dq2[:CONT], dq2[CONT:]).astype(b16)
                dko.append(dot(ds2, qs, TN).astype(b16))
                dvo.append(dot(p2, dcs, TN).astype(b16))
                qall.append(qs)
                dcall.append(dcs)
            span = slice(pair * 2 * rows, (pair + 1) * 2 * rows)
            dkp = dot(ds[...], jnp.concatenate(qall, 0), TN).astype(b16)
            dvp = dot(p_ref[0, span, :PROMPT], jnp.concatenate(dcall, 0), TN).astype(b16)
            dks.append(jnp.concatenate([dkp] + dko, 0))
            dvs.append(jnp.concatenate([dvp] + dvo, 0))
        dkv = jnp.concatenate(dks + dvs, 1)
        dq = dqs[...]
        weight_out(0, dq, a_ref[PROMPT:tall])
        weight_out(1, dkv, a_ref[...])
        acc[...] += dot(dkv, jnp.concatenate([w_ref[0, 1], w_ref[0, 2]], 1), NT)
        acc[PROMPT:] += dot(dq, w_ref[0, 0], NT)

        if not opens:
            @pl.when(step == count - 1)
            def _():
                first_out[:PROMPT] = acc[:PROMPT].astype(b16)
                if padded > PROMPT:
                    first_out[PROMPT:] = jnp.zeros((padded - PROMPT, width), b16)
                row_out[...] = acc[PROMPT:]
                total = jnp.sum(acc[...] * a_ref[...].astype(f32), 0, keepdims=True)
                sums_ref, router_ref = rest_refs
                rows_out = jnp.concatenate(
                    [total / gain_ref[0:1], sums_ref[0:1], router_ref[...], jnp.zeros((SMALL_ROWS - 10, width), f32)], 0
                )
                cut_out(slice(count * 4 * cols, count * 4 * cols + SMALL_ROWS), rows_out.astype(b16))

    def by_group(i, me):
        return (0, base + i)

    row_spec = pl.BlockSpec((rows, width), whole)
    half_spec = pl.BlockSpec((rows // 2, width), whole)
    tall_spec = pl.BlockSpec((tall, width), whole)
    lines = count * 4 * cols + (0 if opens else SMALL_ROWS)
    if opens:
        first_spec, first_shape = tall_spec, jax.ShapeDtypeStruct((tall, width), f32)
    else:
        first_spec, first_shape = pl.BlockSpec((padded, width), whole), jax.ShapeDtypeStruct((padded, width), b16)
    return pl.pallas_call(
        body,
        grid_spec=pltpu.PrefetchScalarGridSpec(
            num_scalar_prefetch=1,
            grid=(count,),
        in_specs=([row_spec] * 4 + [half_spec] * 2 if opens else [row_spec, tall_spec])
        + [
            pl.BlockSpec(gains.shape, whole),
            tall_spec,
            pl.BlockSpec((rows, cols), by_group),
            pl.BlockSpec((tall, cols), by_group),
            pl.BlockSpec((tall, cols), by_group),
            pl.BlockSpec((1, 2 * pairs * rows, keys), lambda i, me: (base + i, 0, 0)),
            pl.BlockSpec((1, 2 * CONT, 128), lambda i, me: (base + i, 0, 0)),
            pl.BlockSpec((rows, cols), by_group),
            pl.BlockSpec((1, 4, width, cols), lambda i, me: (base + i, 0, 0, 0)),
        ]
        + [pl.BlockSpec((8, width), whole)] * len(rest),
        out_specs=[pl.BlockSpec((places, lines, lanes_out), lambda i, me: (0, 0, 0))] * 2
        + [first_spec, row_spec]
        + ([pl.BlockSpec((8, width), whole)] if opens else []),
        scratch_shapes=[
            pltpu.VMEM((rows, width), b16),
            pltpu.VMEM((2 * rows, PROMPT), b16),
            pltpu.VMEM((rows, cols), b16),
            pltpu.VMEM((cols, width), b16),
        ]
        + ([] if opens else [pltpu.VMEM((tall, width), f32)]),
        ),
        out_shape=[
            jax.ShapeDtypeStruct((places, lines, lanes_out), b16),
            jax.ShapeDtypeStruct((places, lines, lanes_out), b16),
            first_shape,
            jax.ShapeDtypeStruct((rows, width), f32),
        ]
        + ([jax.ShapeDtypeStruct((8, width), f32)] if opens else []),
        compiler_params=params(60),
        cost_estimate=pl.CostEstimate(
            flops=count * (width * width * (2 * tall + 2 * rows) + 4 * rows * keys * width) // ESTIMATE,
            bytes_accessed=count * 20 * MIB // ESTIMATE,
            transcendentals=0,
        ),
    )(me, *given, gains, a, q, k, v, p, inv, c, weights, *rest)


def experts_blocks(blocks, given, begun, place, keep, router, weights, start, own, experts, ends):
    width, one = router.shape[0], given[0].shape[0] // (2 if ends else 1)
    units = weights.shape[1]
    n_given, n_begun = len(given), len(begun)
    met = range(start // own, (start + units - 1) // own + 1)

    def body(blocks_ref, *refs):
        given_refs = refs[:n_given]
        keep_ref, r_ref, wg_ref, wu_ref, wd_ref = refs[n_given + n_begun : n_given + n_begun + 5]
        refs = refs[n_given + n_begun + 5 :]
        b_v, dy_v, keep = given_refs[0][...], given_refs[1][...], keep_ref[...]
        if ends:
            y_ref, db_ref, rg_ref, z_ref, dg_ref, du_ref = refs
        else:
            b_ref, dy_ref, y_ref, db_ref, dgates_ref, z_ref, dg_ref, du_ref = refs
            b_ref[...] = b_v
            dy_ref[...] = dy_v
        lane = lax.broadcasted_iota(jnp.int32, (one, 128), 1)
        col = lax.broadcasted_iota(jnp.int32, (one, units), 1)
        logits = dot(b_v, r_ref[...], NN)
        live = lane < experts
        top = jnp.max(jnp.where(live, logits, MASKED), -1, keepdims=True)
        grown = jnp.exp(jnp.where(lane < 2 * experts, logits, MASKED) - top)
        share = grown / jnp.sum(jnp.where(live, grown, 0.0), -1, keepdims=True)
        gates = share.astype(b16).astype(f32) * keep

        g = dot(b_v, wg_ref[0], NT)
        u = dot(b_v, wu_ref[0], NT)
        dz_plain = dot(dy_v, wd_ref[0], NT)
        gate = gates[:, met[-1] : met[-1] + 1]
        for expert in met[-2::-1]:
            gate = jnp.where(col < (expert + 1) * own - start, gates[:, expert : expert + 1], gate)
        cdf, pdf = normal(g)
        act = g * cdf
        z = (act * u).astype(b16).astype(f32)
        along = dz_plain * z
        dgates = given_refs[4][...] if ends else jnp.zeros((one, 128), f32)
        for expert in met:
            low, high = max(expert * own - start, 0), min((expert + 1) * own - start, units)
            inner_low, inner_high = -(-low // 128) * 128, high // 128 * 128
            part = jnp.sum(along[:, inner_low:inner_high], -1, keepdims=True)
            if low < inner_low:
                edge = along[:, inner_low - 128 : inner_low]
                part += jnp.sum(jnp.where(lane >= low % 128, edge, 0.0), -1, keepdims=True)
            if inner_high < high:
                edge = along[:, inner_high : inner_high + 128]
                part += jnp.sum(jnp.where(lane < high % 128, edge, 0.0), -1, keepdims=True)
            dgates += jnp.where(lane % experts == expert, part, 0.0)
        dz = dz_plain * gate
        dg = (dz * u * (cdf + g * pdf)).astype(b16)
        du = (dz * act).astype(b16)
        zg = (z * gate).astype(b16)
        z_ref[...] = zg
        dg_ref[...] = dg
        du_ref[...] = du
        y = dot(zg, wd_ref[0], NN)
        db = dot(dg, wg_ref[0], NN) + dot(du, wu_ref[0], NN)
        if not ends:
            y_ref[...] = y
            db_ref[...] = db
            dgates_ref[...] = dgates
        else:
            dprob = dgates * keep
            inner = jnp.sum(jnp.where(lane < experts, share * dprob, 0.0), -1, keepdims=True)
            dl = jnp.where(lane < 2 * experts, share * (dprob - inner), 0.0)
            head = dl.astype(b16).astype(f32)
            split = jnp.where(lane < experts, head, dl - head).astype(b16)
            rg_ref[0] = dot(b_v, split, TN)
            y_ref[0] = (y + given_refs[2][...]).astype(b16)
            db_ref[0] = (db + given_refs[3][...] + dot(split, r_ref[...], NT)).astype(b16)

    def weight(kind):
        return pl.BlockSpec((1, units, width), lambda i, at: (kind, 0, 0))

    def by_place(i, at):
        return (i if ends else place, 0)

    wide = pl.BlockSpec((one, width), by_place)
    thin = pl.BlockSpec((one, 128), by_place)
    hidden = pl.BlockSpec((one, units), by_place)
    hidden_shape = jax.ShapeDtypeStruct((2 * one, units), b16)
    if ends:
        own_block = pl.BlockSpec((1, one, width), lambda i, at: (i, 0, 0))
        outs = [(own_block, jax.ShapeDtypeStruct((2, one, width), b16))] * 2
        outs += [(pl.BlockSpec((1, width, 128), lambda i, at: (i, 0, 0)), jax.ShapeDtypeStruct((2, width, 128), f32))]
    else:
        outs = [(wide, jax.ShapeDtypeStruct((2 * one, width), b16))] * 2
        outs += [(wide, jax.ShapeDtypeStruct((2 * one, width), f32))] * 2
        outs += [(thin, jax.ShapeDtypeStruct((2 * one, 128), f32))]
    outs += [(hidden, hidden_shape)] * 3
    return pl.pallas_call(
        body,
        grid_spec=pltpu.PrefetchScalarGridSpec(
            num_scalar_prefetch=1,
            grid=(2 if ends else 1,),
            in_specs=([wide] * 4 + [thin] if ends else [pl.BlockSpec((one, width), whole)] * 2)
            + [pl.BlockSpec(memory_space=pl.ANY)] * n_begun
            + [
                pl.BlockSpec((one, 128), lambda i, at: (at[i], 0)),
                pl.BlockSpec((width, 128), whole),
                weight(0),
                weight(1),
                weight(2),
            ],
            out_specs=[spec for spec, _ in outs],
        ),
        out_shape=[shape for _, shape in outs],
        input_output_aliases={1 + n_given + n: n for n in range(n_begun)},
        compiler_params=params(60),
        cost_estimate=pl.CostEstimate(
            flops=(24 if ends else 12) * one * width * units // ESTIMATE,
            bytes_accessed=(6 * units * width + 6 * one * units) // ESTIMATE,
            transcendentals=2 * one * units,
        ),
    )(blocks, *given, *begun, keep, router, weights, weights, weights)


def experts_weights(me, bs, dys, zs, dgs, dus, parts):
    pieces = len(bs)
    rows, width = bs[0].shape
    units = zs[0].shape[1]
    chunk = UNIT_CHUNK
    cut = width // parts
    blocked = cut % 128 == 0

    def body(me_ref, *refs):
        b_refs, dy_refs, z, dg, du = (refs[n * pieces : (n + 1) * pieces] for n in range(5))
        near, far, held = refs[5 * pieces :]
        for kind, (left, right) in enumerate(((dg, b_refs), (du, b_refs), (z, dy_refs))):
            value = dot(left[0][...], right[0][...], TN)
            for n in range(1, pieces):
                value += dot(left[n][...], right[n][...], TN)
            held[kind] = value.astype(b16)
            for s in range(parts if blocked else 0):
                lanes = pl.ds(pl.multiple_of((me_ref[0] ^ s) * cut, cut), cut)
                (far if s % 2 else near)[s // 2, kind] = held[kind, :, lanes]
            if not blocked:
                near[0, kind] = held[kind, :, : width // 2]
                far[0, kind] = held[kind, :, width // 2 :]

    places, lanes = (parts // 2, cut) if blocked else (1, width // 2)
    return pl.pallas_call(
        body,
        grid_spec=pltpu.PrefetchScalarGridSpec(
            num_scalar_prefetch=1,
            grid=(units // chunk,),
            in_specs=[pl.BlockSpec((rows, width), whole)] * (2 * pieces)
            + [pl.BlockSpec((rows, chunk), lambda i, me: (0, i))] * (3 * pieces),
            out_specs=[pl.BlockSpec((places, 3, chunk, lanes), lambda i, me: (0, 0, i, 0))] * 2,
            scratch_shapes=[pltpu.VMEM((3, chunk, width), b16)],
        ),
        out_shape=[jax.ShapeDtypeStruct((places, 3, units, lanes), b16)] * 2,
        compiler_params=params(56),
        cost_estimate=pl.CostEstimate(
            flops=(6 * pieces * rows * width * units) // ESTIMATE,
            bytes_accessed=(6 * units * width + 6 * pieces * rows * units) // ESTIMATE,
            transcendentals=0,
        ),
    )(me, *bs, *dys, *zs, *dgs, *dus)


class Halving:
    def __init__(self, near, other, low, high):
        places = near.shape[0]
        half = (high - low) // 2
        bits = [1 << n for n in range(places.bit_length() - 1)]
        self.orders = [bits, bits[::-1]]
        self.held = []
        for path in range(2):
            span = slice(low + path * half, low + (path + 1) * half)
            self.held.append({s: near[s, span].astype(f32) + other[s, span].astype(f32) for s in range(places)})

    def sends(self):
        self.bits = [order.pop(0) for order in self.orders]
        out = []
        for held, bit in zip(self.held, self.bits):
            out.append((jnp.concatenate([held[s] for s in held if s & bit], 0).astype(b16), 2 * bit, "dp"))
        return out

    def take(self, got):
        for path, (held, bit, came) in enumerate(zip(self.held, self.bits, got)):
            away = [s for s in held if s & bit]
            size = came.shape[0] // len(away)
            self.held[path] = {s ^ bit: held[s ^ bit] + came[n * size : (n + 1) * size].astype(f32) for n, s in enumerate(away)}

    def result(self):
        return jnp.concatenate([held[0] for held in self.held], 0)


def input_gradient(dh, own, piece, sent, x, gains):
    rows, width = dh.shape

    def body(dh_ref, own_ref, piece_ref, sent_ref, x_ref, gain_ref, out_ref):
        da = own_ref[...] + (piece_ref[...].astype(f32) + sent_ref[...].astype(f32))
        unit, scale = unit_of(x_ref[...].astype(f32))
        along = da * gain_ref[0:1]
        inner = jnp.mean(along * unit, -1, keepdims=True)
        out_ref[...] = dh_ref[...] + scale * (along - unit * inner)

    block = pl.BlockSpec((CONT, width), lambda i: (i, 0))
    return pl.pallas_call(
        body,
        grid=(rows // CONT,),
        in_specs=[block] * 5 + [pl.BlockSpec(gains.shape, whole)],
        out_specs=block,
        out_shape=jax.ShapeDtypeStruct((rows, width), f32),
        compiler_params=params(32),
    )(dh, own, piece, sent, x, gains)


def on_device(inputs, cotangent, attn_gain, moe_gain, router, w_query, w_key, w_value, w_out, w_gate, w_up, w_down, expert_ids, priority):
    rows, width = inputs.shape
    experts, cut, own_units = w_gate.shape
    units = experts * own_units
    dp = lax.axis_size("dp")
    depth = lax.axis_size("tensor")
    own = lax.axis_index("tensor")
    me = lax.axis_index("dp")
    at = jnp.full((1,), own, jnp.int32)
    here = jnp.full((1,), me, jnp.int32)
    up = [(i, i + 1) for i in range(depth - 1)]
    down = [(i + 1, i) for i in range(depth - 1)]
    together = lax.optimization_barrier

    def swap(value, bits, axis="tensor"):
        size = depth if axis == "tensor" else dp
        return lax.ppermute(value, axis, [(i, i ^ bits) for i in range(size)])

    def raised(value):
        return lax.ppermute(value, "tensor", up)

    mine = jnp.stack([w_query, w_key, w_value, w_out.T])
    far = swap(mine, 2)
    attention_w = jnp.stack([mine, swap(mine, 1), far, swap(far, 1)])
    attention_w = lax.all_gather(attention_w, "dp", axis=2, tiled=True)

    small = jnp.concatenate([attn_gain[None], moe_gain[None], router.T, jnp.zeros((2, router.shape[0]), b16)], 0)

    def doubled(small, other, index, bit):
        return jnp.where(index & bit != 0, jnp.concatenate([other, small], 1), jnp.concatenate([small, other], 1))

    for bit in [1 << n for n in range(dp.bit_length() - 1)]:
        small = doubled(small, swap(small, bit, "dp"), me, bit)
    x1, other = together((raised(inputs), swap(small, 1)))
    small = doubled(small, other, own, 1)
    x2, other = together((raised(x1), swap(small, 2)))
    small = doubled(small, other, own, 2)
    small = small.reshape(8, depth, dp, -1).swapaxes(1, 2).reshape(8, width)
    x3 = raised(x2)
    gains = small.astype(f32)
    router_full = small[2 : 2 + experts].T
    router_wide = jnp.concatenate(
        [router_full, router_full, jnp.zeros((width, 128 - 2 * experts), b16)], 1
    )
    keep = keep_mask(expert_ids.T, priority.reshape(-1, 2).T, experts)

    shards = [w_gate.transpose(0, 2, 1), w_up.transpose(0, 2, 1), w_down]
    shards = jnp.stack([shard.reshape(units, cut) for shard in shards])
    middle = FIRST_CHUNKS * UNIT_CHUNK
    halves = [
        lax.all_gather(piece, "dp", axis=2, tiled=True)
        for piece in (shards[:, :middle], shards[:, middle:])
    ]

    x3, gains, dy0, keep, router_wide = together((x3, gains, cotangent, keep, router_wide))
    dy1, dy2 = swap(dy0, 1), swap(dy0, 2)
    a, q, k, v, p, inv, c, h, b = attention_forward(at, (inputs, x1, x2, x3), gains, attention_w)
    b, dy1, dy2 = together((b, dy1, dy2))
    b1, b2 = swap(b, 1), swap(b, 2)
    bs, dys = [b], [dy0]

    def open_block(slot, begun):
        block = jnp.full((1,), own ^ slot, jnp.int32)
        return experts_blocks(block, (bs[slot], dys[slot]), begun, slot % 2, keep, router_wide, halves[0], 0, own_units, experts, False)

    def close_pair(pair, given):
        blocks = jnp.stack([own ^ (2 * pair), own ^ (2 * pair + 1)]).astype(jnp.int32)
        return experts_blocks(blocks, given, (), 0, keep, router_wide, halves[1], middle, own_units, experts, True)

    opened_0 = open_block(0, ())
    opened_0, b2 = together((opened_0, b2))
    bs += [b1, b2, swap(b2, 1)]
    dys += [dy1, dy2, swap(dy2, 1)]
    opened_0 = open_block(1, opened_0)
    opened_1 = open_block(3, open_block(2, ()))
    opened_0, opened_1 = together((opened_0, opened_1))
    closed_1 = close_pair(1, opened_1[:5])
    opened_0, closed_1 = together((opened_0, closed_1))
    near3 = swap(closed_1[1][1], 1)
    closed_0 = close_pair(0, opened_0[:5])
    closed_0, near3 = together((closed_0, near3))
    joined = [opened_0[0], opened_1[0]], [opened_0[1], opened_1[1]]
    blocked = cut % 128 == 0

    def stage(sends, given=(), work=None):
        values, given = together((tuple(value for value, *_ in sends), given))
        got = tuple(swap(value, *how) if how else lax.ppermute(value, "tensor", down) for value, (_, *how) in zip(values, sends))
        return together((got, work(given) if work else given))

    def joint(*halvings):
        lists = {}
        for halving in halvings:
            if halving is not None and halving.orders[0]:
                for path, (value, *how) in enumerate(halving.sends()):
                    lists.setdefault(tuple(how), []).append((halving, path, value))
        sends = [(jnp.concatenate([value for *_, value in items], 0), *how) for how, items in lists.items()]

        def take(got):
            came = {}
            for whole_value, items in zip(got, lists.values()):
                start = 0
                for halving, path, value in items:
                    came.setdefault(id(halving), (halving, {}))[1][path] = whole_value[start : start + value.shape[0]]
                    start += value.shape[0]
            for halving, paths in came.values():
                halving.take([paths[0], paths[1]])

        return sends, take

    def flat(value):
        return value.reshape(value.shape[0], -1, value.shape[-1])

    def weights_of(units):
        hidden = (opened_0[5:], opened_1[5:]) if units == 0 else (closed_0[3:], closed_1[3:])
        return lambda given: [flat(v) for v in experts_weights(here, *given, *zip(*hidden), dp)]

    def core_send(far):
        return [(far, 1, "dp")] if blocked else []

    def halving_of(near, got):
        return Halving(near, got[0], 0, near.shape[1]) if blocked else None

    d2 = closed_1[1][0] + near3
    half = rows // 2
    got, (near_0, far_0) = stage([(d2[:half], 2), (closed_1[0][1], 1)], joined, weights_of(0))
    d2_low, near3 = got
    y2 = closed_1[0][0] + near3
    sends = core_send(far_0)
    got, (near_1, far_1) = stage([(closed_0[1][1], 1), (d2[half:], 2)] + sends, joined, weights_of(1))
    d1, d2_high = got[:2]
    units_0 = halving_of(near_0, got[2:])

    rg = (closed_0[2] + closed_1[2]).sum(0)
    rg = (rg[:, :experts] + rg[:, experts : 2 * experts]).T
    rg = jnp.concatenate([rg, jnp.zeros((8 - experts, width), f32)], 0)

    def backward(base, rest):
        return lambda given: attention_backward(here, base, 2, given, rest, gains, a, q, k, v, p, inv, c, attention_w, dp)

    given = (h, cotangent, closed_0[1][0], d1, d2_low, d2_high)
    sends, take = joint(units_0)
    got, opened = stage([(closed_0[0][1], 1)] + core_send(far_1) + sends, given, backward(0, ()))
    y1 = got[0]
    units_1 = halving_of(near_1, got[1:])
    take(got[2:])
    sends, take = joint(units_1, units_0)
    got, closed = stage([(y2, 2)] + core_send(opened[1]) + sends, (opened[3], opened[2]), backward(2, (opened[4], rg)))
    y2 = got[0]
    heads_0 = halving_of(opened[0], got[1:])
    take(got[2:])
    dap, dao, dh = closed[2], closed[3], opened[3]

    def chunk_of(index):
        start = jnp.clip(index, 0, dap.shape[0] // rows - 1) * rows
        piece = lax.dynamic_slice_in_dim(dap, start, rows, 0)
        valid = (index >= 0) & (index < dap.shape[0] // rows)
        return jnp.where(valid, piece, jnp.zeros((), b16))

    sends, take = joint(units_1, heads_0)
    got, _ = stage([(chunk_of(own - depth + 1),)] + core_send(closed[1]) + sends)
    sent = got[0]
    heads_1 = halving_of(closed[0], got[1:])
    take(got[2:])
    sends, take = joint(heads_1, heads_0)
    got, _ = stage([(chunk_of(own - depth + 2) + sent,)] + sends)
    sent = got[0]
    take(got[1:])
    sends, take = joint(heads_1)
    got, _ = stage([(chunk_of(own - depth + 3) + sent,)] + sends)
    sent = got[0]
    take(got[1:])
    if blocked:
        for halving in (units_0, units_1, heads_0, heads_1):
            while halving.orders[0]:
                halving.take([swap(*send) for send in halving.sends()])
        heads_0, heads_1 = heads_0.result(), heads_1.result()
        total_units = jnp.concatenate([part.result().reshape(3, -1, cut) for part in (units_0, units_1)], 1)
    else:
        def summed(near, far):
            return lax.psum_scatter(jnp.concatenate([near[0], far[0]], -1), "dp", scatter_dimension=1, tiled=True)

        heads_0, heads_1 = summed(*opened[:2]), summed(*closed[:2])
        total_units = [summed(*pair).reshape(3, -1, cut) for pair in ((near_0, far_0), (near_1, far_1))]
        total_units = jnp.concatenate(total_units, 1).astype(f32)

    cols = attention_w.shape[-1]
    lines = 4 * cols
    count = width // (dp * depth)

    def slot_of(s):
        head = (heads_0, heads_1)[s // 2][s % 2 * lines : (s % 2 + 1) * lines]
        share = lax.dynamic_slice_in_dim(heads_1[2 * lines :], (own ^ s) * count, count, 1)
        share = jnp.pad(share, ((0, 0), (0, head.shape[1] - count)))
        return jnp.concatenate([head, share], 0)

    total = slot_of(0).astype(f32)
    for s in range(1, depth):
        total = total + swap(slot_of(s).astype(b16), s).astype(f32)
    small_grad = total[lines : lines + 2 + experts, :count]
    total = total[:lines].reshape(4, cols, -1)
    input_grad = input_gradient(dh, dao, chunk_of(own), sent, inputs, gains)
    output = h + closed_0[0][0].astype(f32) + y1.astype(f32) + y2.astype(f32)

    wg_grad, wu_grad, wd_grad = (total_units[n].reshape(experts, own_units, cut) for n in range(3))
    return (
        output.astype(b16),
        input_grad,
        small_grad[0],
        small_grad[1],
        small_grad[2:].T,
        total[0].T,
        total[1].T,
        total[2].T,
        total[3],
        wg_grad.transpose(0, 2, 1),
        wu_grad.transpose(0, 2, 1),
        wd_grad,
    )


def solution(mesh):
    tokens = P(("dp", "tensor"), None)
    vector = P(("dp", "tensor"))
    return jax.shard_map(
        on_device,
        mesh=mesh,
        in_specs=(tokens, tokens, vector, vector, tokens)
        + (P("dp", "tensor"),) * 3
        + (P("tensor", "dp"), P(None, "dp", "tensor"), P(None, "dp", "tensor"), P(None, "tensor", "dp"))
        + (P("dp", None), P("dp", None)),
        out_specs=(tokens, tokens, vector, vector, tokens)
        + (P("dp", "tensor"),) * 3
        + (P("tensor", "dp"), P(None, "dp", "tensor"), P(None, "dp", "tensor"), P(None, "tensor", "dp")),
        check_vma=False,
    )
```

```python
import jax
import jax.numpy as jnp
from jax import lax
from jax.experimental import pallas as pl
from jax.experimental.pallas import tpu as pltpu
from jax.sharding import PartitionSpec as P

HEAD_DIM = 64
PROMPT = 1024
CONT = 128
CAPACITY = 960
EPS = 1e-06
PAIR = 2 * HEAD_DIM
MIB = 2**20

f32 = jnp.float32
b16 = jnp.bfloat16
NN = (((1,), (0,)), ((), ()))
NT = (((1,), (1,)), ((), ()))
TN = (((0,), (0,)), ((), ()))
INV_SQRT2 = 0.7071067811865476
INV_SQRT_2PI = 0.3989422804014327
MASKED = -1e30
SMALL_ROWS = 32
UNIT_CHUNK = 256
ESTIMATE = 4
FIRST_CHUNKS = 6


def dot(left, right, dims):
    return lax.dot_general(left, right, dims, preferred_element_type=f32)


def params(mib):
    return pltpu.CompilerParams(vmem_limit_bytes=mib * MIB)


def whole(*_):
    return (0, 0)


def unit_of(values):
    scale = lax.rsqrt(jnp.mean(values * values, -1, keepdims=True) + EPS)
    return values * scale, scale


def normal(v):
    bell = jnp.exp(-0.5 * v * v)
    t = 1.0 / (1.0 + (0.3275911 * INV_SQRT2) * jnp.abs(v))
    poly = t * (0.127414796 + t * (-0.142248368 + t * (0.710706871 + t * (-0.726576014 + t * 0.530702715))))
    tail = poly * bell
    return jnp.where(v < 0.0, tail, 1.0 - tail), INV_SQRT_2PI * bell


def keep_mask(ids, order, experts):
    rows = ids.shape[1]
    pairs = ids.shape[0] * rows
    bits = pairs.bit_length()

    def body(ids_ref, order_ref, keep_ref):
        ids_v = ids_ref[...]
        order_v = order_ref[...]
        sub = lax.broadcasted_iota(jnp.int32, (128, rows), 0)
        out = jnp.zeros((128, rows), f32)
        for expert in range(experts):
            mine = ids_v == expert
            bound = jnp.zeros((1, 1), jnp.int32)
            for bit in range(bits - 1, -1, -1):
                trial = bound + (1 << bit)
                inside = jnp.where(mine & (order_v < trial), 1.0, 0.0)
                count = jnp.sum(jnp.sum(inside, 1, keepdims=True), 0, keepdims=True)
                bound = jnp.where(count <= CAPACITY, trial, bound)
            kept = jnp.sum(jnp.where(mine & (order_v < bound), 1.0, 0.0), 0, keepdims=True)
            out = jnp.where((sub < 2 * experts) & (sub % experts == expert), kept, out)
        keep_ref[...] = jnp.transpose(out)

    return pl.pallas_call(
        body,
        out_shape=jax.ShapeDtypeStruct((rows, 128), f32),
        compiler_params=params(32),
    )(ids, order)


def attention_forward(at, slots, gains, weights):
    rows, width = slots[0].shape
    groups, _, _, cols = weights.shape
    tall = PROMPT + rows
    subs = rows // CONT
    pairs = cols // PAIR
    keys = PROMPT + CONT

    def body(at_ref, x0, x1, x2, x3, gain_ref, w_ref, a_out, q_ref, k_ref, v_ref, p_ref, inv_ref, c_ref, h_ref, b_ref, xs, acc, a_s, a_sem):
        step = pl.program_id(0)
        t = at_ref[0]
        a_ref = a_s
        store = pltpu.make_async_copy(a_s, a_out, a_sem)

        @pl.when(step == 0)
        def _():
            for s, x in enumerate((x0, x1, x2, x3)):
                xs[s * rows : (s + 1) * rows] = x[...]
            gain = gain_ref[0:1]
            for start in range(0, PROMPT, rows):
                take = min(rows, PROMPT - start)
                slot = jnp.maximum(t - start // rows, 0)
                x = xs[pl.ds(pl.multiple_of(slot * rows, 128), take)].astype(f32)
                a_ref[start : start + take] = (unit_of(x)[0] * gain).astype(b16)
            x = x0[...].astype(f32)
            a_ref[PROMPT:tall] = (unit_of(x)[0] * gain).astype(b16)
            acc[...] = x
            store.start()

        q = dot(a_ref[PROMPT:tall], w_ref[0, 0], NN).astype(b16) * jnp.asarray(0.125, b16)
        kv = dot(a_ref[...], jnp.concatenate([w_ref[0, 1], w_ref[0, 2]], 1), NN).astype(b16)
        k, v = kv[:, :cols], kv[:, cols:]
        q_ref[...] = q
        k_ref[...] = k
        v_ref[...] = v
        low = lax.broadcasted_iota(jnp.int32, (CONT, PAIR), 1) < HEAD_DIM
        row = lax.broadcasted_iota(jnp.int32, (2 * CONT, PROMPT), 0) % CONT
        past = lax.broadcasted_iota(jnp.int32, (2 * CONT, PROMPT), 1) - row
        own_ok = lax.broadcasted_iota(jnp.int32, (2 * CONT, CONT), 1) <= (
            lax.broadcasted_iota(jnp.int32, (2 * CONT, CONT), 0) % CONT
        )
        lane = lax.broadcasted_iota(jnp.int32, (2 * CONT, 128), 1)
        inverses = jnp.zeros((2 * CONT, 128), f32)
        zero = jnp.zeros((), b16)
        for pair in range(pairs):
            lanes = slice(pair * PAIR, (pair + 1) * PAIR)
            kp, vp = k[:PROMPT, lanes], v[:PROMPT, lanes]
            for sub in range(subs):
                unit = pair * subs + sub
                own = slice(PROMPT + sub * CONT, PROMPT + (sub + 1) * CONT)
                q2 = q[sub * CONT : (sub + 1) * CONT, lanes]
                qs = jnp.concatenate([jnp.where(low, q2, zero), jnp.where(low, zero, q2)], 0)
                first = t * rows + sub * CONT
                s1 = jnp.where(past <= first, dot(qs, kp, NT), MASKED)
                s2 = jnp.where(own_ok & (first >= PROMPT), dot(qs, k[own, lanes], NT), MASKED)
                top = jnp.maximum(jnp.max(s1, -1, keepdims=True), jnp.max(s2, -1, keepdims=True))
                e1 = jnp.exp(s1 - top)
                e2 = jnp.exp(s2 - top)
                inv = 1.0 / (jnp.sum(e1, -1, keepdims=True) + jnp.sum(e2, -1, keepdims=True))
                inverses = jnp.where(lane == unit, inv, inverses)
                p1 = e1.astype(b16)
                p2 = e2.astype(b16)
                at_p = slice(unit * 2 * CONT, (unit + 1) * 2 * CONT)
                p_ref[0, at_p, :PROMPT] = p1
                p_ref[0, at_p, PROMPT:] = p2
                c2 = (dot(p1, vp, NN) + dot(p2, v[own, lanes], NN)) * inv
                c_ref[sub * CONT : (sub + 1) * CONT, lanes] = jnp.where(low, c2[:CONT], c2[CONT:]).astype(b16)
        inv_ref[0] = inverses
        acc[...] += dot(c_ref[...], w_ref[0, 3], NT)

        @pl.when(step == groups - 1)
        def _():
            store.wait()
            h = acc[...]
            h_ref[...] = h
            b_ref[...] = (unit_of(h)[0] * gain_ref[1:2]).astype(b16)

    def by_group(i, at):
        return (0, i)

    return pl.pallas_call(
        body,
        grid_spec=pltpu.PrefetchScalarGridSpec(
            num_scalar_prefetch=1,
            grid=(groups,),
            in_specs=[pl.BlockSpec((rows, width), whole)] * 4
            + [
                pl.BlockSpec(gains.shape, whole),
                pl.BlockSpec((1, 4, width, cols), lambda i, at: (i, 0, 0, 0)),
            ],
            out_specs=[
                pl.BlockSpec(memory_space=pl.ANY),
                pl.BlockSpec((rows, cols), by_group),
                pl.BlockSpec((tall, cols), by_group),
                pl.BlockSpec((tall, cols), by_group),
                pl.BlockSpec((1, 2 * pairs * rows, keys), lambda i, at: (i, 0, 0)),
                pl.BlockSpec((1, 2 * CONT, 128), lambda i, at: (i, 0, 0)),
                pl.BlockSpec((rows, cols), by_group),
                pl.BlockSpec((rows, width), whole),
                pl.BlockSpec((rows, width), whole),
            ],
            scratch_shapes=[
                pltpu.VMEM((4 * rows, width), b16),
                pltpu.VMEM((rows, width), f32),
                pltpu.VMEM((tall, width), b16),
                pltpu.SemaphoreType.DMA,
            ],
        ),
        out_shape=[
            jax.ShapeDtypeStruct((tall, width), b16),
            jax.ShapeDtypeStruct((rows, width), b16),
            jax.ShapeDtypeStruct((tall, width), b16),
            jax.ShapeDtypeStruct((tall, width), b16),
            jax.ShapeDtypeStruct((groups, 2 * pairs * rows, keys), b16),
            jax.ShapeDtypeStruct((groups, 2 * CONT, 128), f32),
            jax.ShapeDtypeStruct((rows, width), b16),
            jax.ShapeDtypeStruct((rows, width), f32),
            jax.ShapeDtypeStruct((rows, width), b16),
        ],
        compiler_params=params(56),
        cost_estimate=pl.CostEstimate(
            flops=(2 * width * width * (2 * tall + 2 * rows) + 8 * rows * keys * width) // ESTIMATE,
            bytes_accessed=60 * MIB // ESTIMATE,
            transcendentals=rows * keys * 16,
        ),
    )(at, *slots, gains, weights)


def attention_backward(me, base, count, given, rest, gains, a, q, k, v, p, inv, c, weights, parts):
    opens = base == 0
    rows, width = q.shape
    _, _, _, cols = weights.shape
    tall = PROMPT + rows
    padded = -(-PROMPT // rows) * rows
    subs = rows // CONT
    pairs = cols // PAIR
    keys = PROMPT + CONT
    cut = width // parts
    blocked = cut % 128 == 0
    places, lanes_out = (parts // 2, cut) if blocked else (1, width // 2)

    def body(me_ref, *refs):
        n_given = 6 if opens else 2
        given_refs = refs[:n_given]
        gain_ref, a_ref, q_ref, k_ref, v_ref, p_ref, inv_ref, c_ref, w_ref = refs[n_given : n_given + 9]
        rest_refs = refs[n_given + 9 : n_given + 9 + len(rest)]
        refs = refs[n_given + 9 + len(rest) :]
        near, far, first_out, row_out, *refs = refs
        if opens:
            sum_ref, *refs = refs
        do, ds, dqs, held, *more = refs
        step = pl.program_id(0)
        acc = more[0]

        @pl.when(step == 0)
        def _():
            if opens:
                h_ref, dy_ref, *part_refs = given_refs
                d0, d1 = (r[...].astype(f32) for r in part_refs[:2])
                dn = d0 + d1 + jnp.concatenate([r[...] for r in part_refs[2:]], 0).astype(f32)
                gain = gain_ref[1:2]
                unit, scale = unit_of(h_ref[...])
                along = dn * gain
                inner = jnp.mean(along * unit, -1, keepdims=True)
                dh = dy_ref[...].astype(f32) + scale * (along - unit * inner)
                row_out[...] = dh
                do[...] = dh.astype(b16)
                sum_ref[...] = jnp.broadcast_to(jnp.sum(dn * unit, 0, keepdims=True), sum_ref.shape)
                acc[...] = jnp.zeros_like(acc)
            else:
                do[...] = given_refs[0][...].astype(b16)
                acc[...] = given_refs[1][...].astype(f32)

        low = lax.broadcasted_iota(jnp.int32, (CONT, PAIR), 1) < HEAD_DIM
        zero = jnp.zeros((), b16)

        def stacked(two):
            return jnp.concatenate([jnp.where(low, two, zero), jnp.where(low, zero, two)], 0)

        def cut_out(start_line, piece):
            count = piece.shape[0]
            span = pl.ds(start_line, count)
            held[:count] = piece
            for s in range(parts if blocked else 2):
                start = (me_ref[0] ^ s) * cut if blocked else s * lanes_out
                lanes = pl.ds(pl.multiple_of(start, lanes_out), lanes_out)
                (far if s % 2 else near)[s // 2, span] = held[:count, lanes]

        def weight_out(kind, left, right, dims):
            value = dot(left, right, dims).astype(b16)
            for n in range(value.shape[0] // cols):
                piece = value[n * cols : (n + 1) * cols]
                line = (kind + n) * cols
                cut_out(line if opens else pl.multiple_of(step * 4 * cols + line, 128), piece)

        dc = dot(do[...], w_ref[0, 3], NN).astype(b16)
        weight_out(3, c_ref[...], do[...], TN)
        dks, dvs = [], []
        for pair in range(pairs):
            lanes = slice(pair * PAIR, (pair + 1) * PAIR)
            kp, vp = k_ref[:PROMPT, lanes], v_ref[:PROMPT, lanes]
            qall, dcall, dko, dvo = [], [], [], []
            for sub in range(subs):
                n = pair * subs + sub
                own = slice(PROMPT + sub * CONT, PROMPT + (sub + 1) * CONT)
                mine = slice(sub * CONT, (sub + 1) * CONT)
                at_p = slice(n * 2 * CONT, (n + 1) * 2 * CONT)
                dcs = (stacked(dc[mine, lanes]).astype(f32) * inv_ref[0][:, n : n + 1]).astype(b16)
                qs = stacked(q_ref[mine, lanes])
                cs = stacked(c_ref[mine, lanes])
                delta = jnp.sum(dcs.astype(f32) * cs.astype(f32), -1, keepdims=True)
                p1 = p_ref[0, at_p, :PROMPT]
                p2 = p_ref[0, at_p, PROMPT:]
                ds1 = (p1.astype(f32) * (dot(dcs, vp, NT) - delta)).astype(b16)
                ds2 = (p2.astype(f32) * (dot(dcs, v_ref[own, lanes], NT) - delta)).astype(b16)
                ds[sub * 2 * CONT : (sub + 1) * 2 * CONT] = ds1
                dq2 = (dot(ds1, kp, NN) + dot(ds2, k_ref[own, lanes], NN)) * 0.125
                dqs[mine, lanes] = jnp.where(low, dq2[:CONT], dq2[CONT:]).astype(b16)
                dko.append(dot(qs, ds2, TN).astype(b16))
                dvo.append(dot(dcs, p2, TN).astype(b16))
                qall.append(qs)
                dcall.append(dcs)
            span = slice(pair * 2 * rows, (pair + 1) * 2 * rows)
            dkp = dot(jnp.concatenate(qall, 0), ds[...], TN).astype(b16)
            dvp = dot(jnp.concatenate(dcall, 0), p_ref[0, span, :PROMPT], TN).astype(b16)
            dks.append(jnp.concatenate([dkp] + dko, 1))
            dvs.append(jnp.concatenate([dvp] + dvo, 1))
        turned = jnp.concatenate(dks + dvs, 0)
        dq = dqs[...]
        weight_out(0, dq, a_ref[PROMPT:tall], TN)
        weight_out(1, turned, a_ref[...], NN)
        acc[...] += dot(jnp.transpose(turned), jnp.concatenate([w_ref[0, 1], w_ref[0, 2]], 1), NT)
        acc[PROMPT:] += dot(dq, w_ref[0, 0], NT)

        @pl.when(step == count - 1)
        def _():
            if opens:
                first_out[...] = acc[...].astype(b16)
            else:
                first_out[:PROMPT] = acc[:PROMPT].astype(b16)
                if padded > PROMPT:
                    first_out[PROMPT:] = jnp.zeros((padded - PROMPT, width), b16)
                row_out[...] = acc[PROMPT:]
                total = jnp.sum(acc[...] * a_ref[...].astype(f32), 0, keepdims=True)
                sums_ref, router_ref = rest_refs
                rows_out = jnp.concatenate(
                    [total / gain_ref[0:1], sums_ref[0:1], router_ref[...], jnp.zeros((SMALL_ROWS - 10, width), f32)], 0
                )
                cut_out(count * 4 * cols, rows_out.astype(b16))

    def by_group(i, me):
        return (0, base + i)

    row_spec = pl.BlockSpec((rows, width), whole)
    half_spec = pl.BlockSpec((rows // 2, width), whole)
    tall_spec = pl.BlockSpec((tall, width), whole)
    lines = count * 4 * cols + (0 if opens else SMALL_ROWS)
    if opens:
        first_spec, first_shape = tall_spec, jax.ShapeDtypeStruct((tall, width), b16)
    else:
        first_spec, first_shape = pl.BlockSpec((padded, width), whole), jax.ShapeDtypeStruct((padded, width), b16)
    return pl.pallas_call(
        body,
        grid_spec=pltpu.PrefetchScalarGridSpec(
            num_scalar_prefetch=1,
            grid=(count,),
        in_specs=([row_spec] * 4 + [half_spec] * 2 if opens else [row_spec, tall_spec])
        + [
            pl.BlockSpec(gains.shape, whole),
            tall_spec,
            pl.BlockSpec((rows, cols), by_group),
            pl.BlockSpec((tall, cols), by_group),
            pl.BlockSpec((tall, cols), by_group),
            pl.BlockSpec((1, 2 * pairs * rows, keys), lambda i, me: (base + i, 0, 0)),
            pl.BlockSpec((1, 2 * CONT, 128), lambda i, me: (base + i, 0, 0)),
            pl.BlockSpec((rows, cols), by_group),
            pl.BlockSpec((1, 4, width, cols), lambda i, me: (base + i, 0, 0, 0)),
        ]
        + [pl.BlockSpec((8, width), whole)] * len(rest),
        out_specs=[
            pl.BlockSpec((places, 4 * cols, lanes_out), lambda i, me: (0, i, 0))
            if opens
            else pl.BlockSpec((places, lines, lanes_out), lambda i, me: (0, 0, 0))
        ]
        * 2
        + [first_spec, row_spec]
        + ([pl.BlockSpec((8, width), whole)] if opens else []),
        scratch_shapes=[
            pltpu.VMEM((rows, width), b16),
            pltpu.VMEM((2 * rows, PROMPT), b16),
            pltpu.VMEM((rows, cols), b16),
            pltpu.VMEM((cols, width), b16),
        ]
        + [pltpu.VMEM((tall, width), f32)],
        ),
        out_shape=[
            jax.ShapeDtypeStruct((places, lines, lanes_out), b16),
            jax.ShapeDtypeStruct((places, lines, lanes_out), b16),
            first_shape,
            jax.ShapeDtypeStruct((rows, width), f32),
        ]
        + ([jax.ShapeDtypeStruct((8, width), f32)] if opens else []),
        compiler_params=params(60),
        cost_estimate=pl.CostEstimate(
            flops=count * (width * width * (2 * tall + 2 * rows) + 4 * rows * keys * width) // ESTIMATE,
            bytes_accessed=count * 20 * MIB // ESTIMATE,
            transcendentals=0,
        ),
    )(me, *given, gains, a, q, k, v, p, inv, c, weights, *rest)


def experts_blocks(blocks, given, begun, place, keep, router, weights, start, own, experts, ends):
    width, one = router.shape[0], given[0].shape[0] // (2 if ends else 1)
    units = weights.shape[1]
    n_given, n_begun = len(given), len(begun)
    met = range(start // own, (start + units - 1) // own + 1)

    def body(blocks_ref, *refs):
        given_refs = refs[:n_given]
        keep_ref, r_ref, wg_ref, wu_ref, wd_ref = refs[n_given + n_begun : n_given + n_begun + 5]
        refs = refs[n_given + n_begun + 5 :]
        b_v, dy_v, keep = given_refs[0][...], given_refs[1][...], keep_ref[...]
        if ends:
            y_ref, db_ref, rg_ref, z_ref, dg_ref, du_ref = refs
        else:
            b_ref, dy_ref, y_ref, db_ref, dgates_ref, z_ref, dg_ref, du_ref = refs
            b_ref[...] = b_v
            dy_ref[...] = dy_v
        lane = lax.broadcasted_iota(jnp.int32, (one, 128), 1)
        col = lax.broadcasted_iota(jnp.int32, (one, units), 1)
        logits = dot(b_v, r_ref[...], NN)
        live = lane < experts
        top = jnp.max(jnp.where(live, logits, MASKED), -1, keepdims=True)
        grown = jnp.exp(jnp.where(lane < 2 * experts, logits, MASKED) - top)
        share = grown / jnp.sum(jnp.where(live, grown, 0.0), -1, keepdims=True)
        gates = share.astype(b16).astype(f32) * keep

        g = dot(b_v, wg_ref[0], NT)
        u = dot(b_v, wu_ref[0], NT)
        dz_plain = dot(dy_v, wd_ref[0], NT)
        gate = gates[:, met[-1] : met[-1] + 1]
        for expert in met[-2::-1]:
            gate = jnp.where(col < (expert + 1) * own - start, gates[:, expert : expert + 1], gate)
        cdf, pdf = normal(g)
        act = g * cdf
        z = (act * u).astype(b16).astype(f32)
        along = dz_plain * z
        dgates = given_refs[4][...] if ends else jnp.zeros((one, 128), f32)
        for expert in met:
            low, high = max(expert * own - start, 0), min((expert + 1) * own - start, units)
            inner_low, inner_high = -(-low // 128) * 128, high // 128 * 128
            part = jnp.sum(along[:, inner_low:inner_high], -1, keepdims=True)
            if low < inner_low:
                edge = along[:, inner_low - 128 : inner_low]
                part += jnp.sum(jnp.where(lane >= low % 128, edge, 0.0), -1, keepdims=True)
            if inner_high < high:
                edge = along[:, inner_high : inner_high + 128]
                part += jnp.sum(jnp.where(lane < high % 128, edge, 0.0), -1, keepdims=True)
            dgates += jnp.where(lane % experts == expert, part, 0.0)
        dz = dz_plain * gate
        dg = (dz * u * (cdf + g * pdf)).astype(b16)
        du = (dz * act).astype(b16)
        zg = (z * gate).astype(b16)
        z_ref[...] = zg
        dg_ref[...] = dg
        du_ref[...] = du
        y = dot(zg, wd_ref[0], NN)
        db = dot(dg, wg_ref[0], NN) + dot(du, wu_ref[0], NN)
        if not ends:
            y_ref[...] = y
            db_ref[...] = db
            dgates_ref[...] = dgates
        else:
            dprob = dgates * keep
            inner = jnp.sum(jnp.where(lane < experts, share * dprob, 0.0), -1, keepdims=True)
            dl = jnp.where(lane < 2 * experts, share * (dprob - inner), 0.0)
            head = dl.astype(b16).astype(f32)
            split = jnp.where(lane < experts, head, dl - head).astype(b16)
            rg_ref[0] = dot(split, b_v, TN)[:8]
            y_ref[0] = (y + given_refs[2][...]).astype(b16)
            db_ref[0] = (db + given_refs[3][...] + dot(split, r_ref[...], NT)).astype(b16)

    def weight(kind):
        return pl.BlockSpec((1, units, width), lambda i, at: (kind, 0, 0))

    def by_place(i, at):
        return (i if ends else place, 0)

    wide = pl.BlockSpec((one, width), by_place)
    thin = pl.BlockSpec((one, 128), by_place)
    hidden = pl.BlockSpec((one, units), by_place)
    hidden_shape = jax.ShapeDtypeStruct((2 * one, units), b16)
    if ends:
        own_block = pl.BlockSpec((1, one, width), lambda i, at: (i, 0, 0))
        outs = [(own_block, jax.ShapeDtypeStruct((2, one, width), b16))] * 2
        outs += [(pl.BlockSpec((1, 8, width), lambda i, at: (i, 0, 0)), jax.ShapeDtypeStruct((2, 8, width), f32))]
    else:
        outs = [(wide, jax.ShapeDtypeStruct((2 * one, width), b16))] * 2
        outs += [(wide, jax.ShapeDtypeStruct((2 * one, width), f32))] * 2
        outs += [(thin, jax.ShapeDtypeStruct((2 * one, 128), f32))]
    outs += [(hidden, hidden_shape)] * 3
    return pl.pallas_call(
        body,
        grid_spec=pltpu.PrefetchScalarGridSpec(
            num_scalar_prefetch=1,
            grid=(2 if ends else 1,),
            in_specs=([wide] * 4 + [thin] if ends else [pl.BlockSpec((one, width), whole)] * 2)
            + [pl.BlockSpec(memory_space=pl.ANY)] * n_begun
            + [
                pl.BlockSpec((one, 128), lambda i, at: (at[i], 0)),
                pl.BlockSpec((width, 128), whole),
                weight(0),
                weight(1),
                weight(2),
            ],
            out_specs=[spec for spec, _ in outs],
        ),
        out_shape=[shape for _, shape in outs],
        input_output_aliases={1 + n_given + n: n for n in range(n_begun)},
        compiler_params=params(60),
        cost_estimate=pl.CostEstimate(
            flops=(24 if ends else 12) * one * width * units // ESTIMATE,
            bytes_accessed=(6 * units * width + 6 * one * units) // ESTIMATE,
            transcendentals=2 * one * units,
        ),
    )(blocks, *given, *begun, keep, router, weights, weights, weights)


def experts_weights(me, bs, dys, zs, dgs, dus, parts):
    pieces = len(bs)
    rows, width = bs[0].shape
    units = zs[0].shape[1]
    chunk = UNIT_CHUNK
    cut = width // parts
    blocked = cut % 128 == 0

    def body(me_ref, *refs):
        b_refs, dy_refs, z, dg, du = (refs[n * pieces : (n + 1) * pieces] for n in range(5))
        near, far, held = refs[5 * pieces :]
        for kind, (left, right) in enumerate(((dg, b_refs), (du, b_refs), (z, dy_refs))):
            value = dot(left[0][...], right[0][...], TN)
            for n in range(1, pieces):
                value += dot(left[n][...], right[n][...], TN)
            held[kind] = value.astype(b16)
            for s in range(parts if blocked else 0):
                lanes = pl.ds(pl.multiple_of((me_ref[0] ^ s) * cut, cut), cut)
                (far if s % 2 else near)[s // 2, kind] = held[kind, :, lanes]
            if not blocked:
                near[0, kind] = held[kind, :, : width // 2]
                far[0, kind] = held[kind, :, width // 2 :]

    places, lanes = (parts // 2, cut) if blocked else (1, width // 2)
    return pl.pallas_call(
        body,
        grid_spec=pltpu.PrefetchScalarGridSpec(
            num_scalar_prefetch=1,
            grid=(units // chunk,),
            in_specs=[pl.BlockSpec((rows, width), whole)] * (2 * pieces)
            + [pl.BlockSpec((rows, chunk), lambda i, me: (0, i))] * (3 * pieces),
            out_specs=[pl.BlockSpec((places, 3, chunk, lanes), lambda i, me: (0, 0, i, 0))] * 2,
            scratch_shapes=[pltpu.VMEM((3, chunk, width), b16)],
        ),
        out_shape=[jax.ShapeDtypeStruct((places, 3, units, lanes), b16)] * 2,
        compiler_params=params(56),
        cost_estimate=pl.CostEstimate(
            flops=(6 * pieces * rows * width * units) // ESTIMATE,
            bytes_accessed=(6 * units * width + 6 * pieces * rows * units) // ESTIMATE,
            transcendentals=0,
        ),
    )(me, *bs, *dys, *zs, *dgs, *dus)


class Halving:
    def __init__(self, near, other, low, high):
        places = near.shape[0]
        half = (high - low) // 2
        bits = [1 << n for n in range(places.bit_length() - 1)]
        self.orders = [bits, bits[::-1]]
        self.held = []
        for path in range(2):
            span = slice(low + path * half, low + (path + 1) * half)
            self.held.append({s: near[s, span].astype(f32) + other[s, span].astype(f32) for s in range(places)})

    def sends(self):
        self.bits = [order.pop(0) for order in self.orders]
        out = []
        for held, bit in zip(self.held, self.bits):
            out.append((jnp.concatenate([held[s] for s in held if s & bit], 0).astype(b16), 2 * bit, "dp"))
        return out

    def take(self, got):
        for path, (held, bit, came) in enumerate(zip(self.held, self.bits, got)):
            away = [s for s in held if s & bit]
            size = came.shape[0] // len(away)
            self.held[path] = {s ^ bit: held[s ^ bit] + came[n * size : (n + 1) * size].astype(f32) for n, s in enumerate(away)}

    def result(self):
        return jnp.concatenate([held[0] for held in self.held], 0)


def input_gradient(dh, own, piece, sent, x, gains):
    rows, width = dh.shape

    def body(dh_ref, own_ref, piece_ref, sent_ref, x_ref, gain_ref, out_ref):
        da = own_ref[...] + (piece_ref[...].astype(f32) + sent_ref[...].astype(f32))
        unit, scale = unit_of(x_ref[...].astype(f32))
        along = da * gain_ref[0:1]
        inner = jnp.mean(along * unit, -1, keepdims=True)
        out_ref[...] = dh_ref[...] + scale * (along - unit * inner)

    block = pl.BlockSpec((CONT, width), lambda i: (i, 0))
    return pl.pallas_call(
        body,
        grid=(rows // CONT,),
        in_specs=[block] * 5 + [pl.BlockSpec(gains.shape, whole)],
        out_specs=block,
        out_shape=jax.ShapeDtypeStruct((rows, width), f32),
        compiler_params=params(32),
    )(dh, own, piece, sent, x, gains)


def on_device(inputs, cotangent, attn_gain, moe_gain, router, w_query, w_key, w_value, w_out, w_gate, w_up, w_down, expert_ids, priority):
    rows, width = inputs.shape
    experts, cut, own_units = w_gate.shape
    units = experts * own_units
    dp = lax.axis_size("dp")
    depth = lax.axis_size("tensor")
    own = lax.axis_index("tensor")
    me = lax.axis_index("dp")
    at = jnp.full((1,), own, jnp.int32)
    here = jnp.full((1,), me, jnp.int32)
    up = [(i, i + 1) for i in range(depth - 1)]
    down = [(i + 1, i) for i in range(depth - 1)]
    together = lax.optimization_barrier

    def swap(value, bits, axis="tensor"):
        size = depth if axis == "tensor" else dp
        return lax.ppermute(value, axis, [(i, i ^ bits) for i in range(size)])

    def raised(value):
        return lax.ppermute(value, "tensor", up)

    mine = jnp.stack([w_query, w_key, w_value, w_out.T])
    far = swap(mine, 2)
    attention_w = jnp.stack([mine, swap(mine, 1), far, swap(far, 1)])
    attention_w = lax.all_gather(attention_w, "dp", axis=2, tiled=True)

    small = jnp.concatenate([attn_gain[None], moe_gain[None], router.T, jnp.zeros((2, router.shape[0]), b16)], 0)

    def doubled(small, other, index, bit):
        return jnp.where(index & bit != 0, jnp.concatenate([other, small], 1), jnp.concatenate([small, other], 1))

    for bit in [1 << n for n in range(dp.bit_length() - 1)]:
        small = doubled(small, swap(small, bit, "dp"), me, bit)
    x1, other = together((raised(inputs), swap(small, 1)))
    small = doubled(small, other, own, 1)
    x2, other = together((raised(x1), swap(small, 2)))
    small = doubled(small, other, own, 2)
    small = small.reshape(8, depth, dp, -1).swapaxes(1, 2).reshape(8, width)
    x3 = raised(x2)
    gains = small.astype(f32)
    router_full = small[2 : 2 + experts].T
    router_wide = jnp.concatenate(
        [router_full, router_full, jnp.zeros((width, 128 - 2 * experts), b16)], 1
    )
    keep = keep_mask(expert_ids.T, priority.reshape(-1, 2).T, experts)

    shards = [w_gate.transpose(0, 2, 1), w_up.transpose(0, 2, 1), w_down]
    shards = jnp.stack([shard.reshape(units, cut) for shard in shards])
    middle = FIRST_CHUNKS * UNIT_CHUNK
    halves = [
        lax.all_gather(piece, "dp", axis=2, tiled=True)
        for piece in (shards[:, :middle], shards[:, middle:])
    ]

    x3, gains, dy0, keep, router_wide = together((x3, gains, cotangent, keep, router_wide))
    dy1, dy2 = swap(dy0, 1), swap(dy0, 2)
    a, q, k, v, p, inv, c, h, b = attention_forward(at, (inputs, x1, x2, x3), gains, attention_w)
    b, dy1, dy2 = together((b, dy1, dy2))
    b1, b2 = swap(b, 1), swap(b, 2)
    bs, dys = [b], [dy0]

    def open_block(slot, begun):
        block = jnp.full((1,), own ^ slot, jnp.int32)
        return experts_blocks(block, (bs[slot], dys[slot]), begun, slot % 2, keep, router_wide, halves[0], 0, own_units, experts, False)

    def close_pair(pair, given):
        blocks = jnp.stack([own ^ (2 * pair), own ^ (2 * pair + 1)]).astype(jnp.int32)
        return experts_blocks(blocks, given, (), 0, keep, router_wide, halves[1], middle, own_units, experts, True)

    opened_0 = open_block(0, ())
    opened_0, b2 = together((opened_0, b2))
    bs += [b1, b2, swap(b2, 1)]
    dys += [dy1, dy2, swap(dy2, 1)]
    opened_0 = open_block(1, opened_0)
    opened_1 = open_block(3, open_block(2, ()))
    opened_0, opened_1 = together((opened_0, opened_1))
    closed_1 = close_pair(1, opened_1[:5])
    opened_0, closed_1 = together((opened_0, closed_1))
    near3 = swap(closed_1[1][1], 1)
    closed_0 = close_pair(0, opened_0[:5])
    closed_0, near3 = together((closed_0, near3))
    joined = [opened_0[0], opened_1[0]], [opened_0[1], opened_1[1]]
    blocked = cut % 128 == 0

    def stage(sends, given=(), work=None):
        values = tuple(value for value, *_ in sends)
        if work is None:
            values = together(values)
        else:
            values, given = together((values, given))
        got = tuple(swap(value, *how) for value, (_, *how) in zip(values, sends))
        return together((got, given if work is None else work(given)))

    def joint(*halvings):
        lists = {}
        for halving in halvings:
            if halving is not None and halving.orders[0]:
                for path, (value, *how) in enumerate(halving.sends()):
                    lists.setdefault(tuple(how), []).append((halving, path, value))
        sends = [(jnp.concatenate([value for *_, value in items], 0), *how) for how, items in lists.items()]

        def take(got):
            came = {}
            for whole_value, items in zip(got, lists.values()):
                start = 0
                for halving, path, value in items:
                    came.setdefault(id(halving), (halving, {}))[1][path] = whole_value[start : start + value.shape[0]]
                    start += value.shape[0]
            for halving, paths in came.values():
                halving.take([paths[0], paths[1]])

        return sends, take

    def flat(value):
        return value.reshape(value.shape[0], -1, value.shape[-1])

    def weights_of(units):
        hidden = (opened_0[5:], opened_1[5:]) if units == 0 else (closed_0[3:], closed_1[3:])
        return lambda given: [flat(v) for v in experts_weights(here, *given, *zip(*hidden), dp)]

    def core_send(far):
        return [(far, 1, "dp")] if blocked else []

    def halving_of(near, got):
        return Halving(near, got[0], 0, near.shape[1]) if blocked else None

    d2 = closed_1[1][0] + near3
    half = rows // 2
    got, (near_0, far_0) = stage([(d2[:half], 2), (closed_1[0][1], 1)], joined, weights_of(0))
    d2_low, near3 = got
    y2 = closed_1[0][0] + near3
    sends = core_send(far_0)
    got, (near_1, far_1) = stage([(closed_0[1][1], 1), (d2[half:], 2)] + sends, joined, weights_of(1))
    d1, d2_high = got[:2]
    units_0 = halving_of(near_0, got[2:])

    rg = (closed_0[2] + closed_1[2]).sum(0)
    rg = jnp.concatenate([rg[:experts] + rg[experts : 2 * experts], jnp.zeros((8 - experts, width), f32)], 0)

    def backward(base, rest):
        return lambda given: attention_backward(here, base, 2, given, rest, gains, a, q, k, v, p, inv, c, attention_w, dp)

    given = (h, cotangent, closed_0[1][0], d1, d2_low, d2_high)
    sends, take = joint(units_0)
    got, opened = stage([(closed_0[0][1], 1)] + core_send(far_1) + sends, given, backward(0, ()))
    y1 = got[0]
    units_1 = halving_of(near_1, got[1:])
    take(got[2:])
    sends, take = joint(units_1, units_0)
    got, closed = stage([(y2, 2)] + core_send(opened[1]) + sends, (opened[3], opened[2]), backward(2, (opened[4], rg)))
    y2 = got[0]
    heads_0 = halving_of(opened[0], got[1:])
    take(got[2:])
    dap, dao, dh = closed[2], closed[3], opened[3]

    def chunk_of(index):
        start = jnp.clip(index, 0, dap.shape[0] // rows - 1) * rows
        piece = lax.dynamic_slice_in_dim(dap, start, rows, 0)
        valid = (index >= 0) & (index < dap.shape[0] // rows)
        return jnp.where(valid, piece, jnp.zeros((), b16))

    def hop(index, sent=None):
        piece = chunk_of(own - depth + index)
        return lax.ppermute(piece if sent is None else piece + sent, "tensor", down)

    sent = hop(1)
    sends, take = joint(units_1, heads_0)
    got, sent = stage(core_send(closed[1]) + sends, sent)
    heads_1 = halving_of(closed[0], got)
    take(got[1:])
    sent = hop(2, sent)
    sends, take = joint(heads_1, heads_0)
    got, sent = stage(sends, sent)
    take(got)
    sent = hop(3, sent)
    sends, take = joint(heads_1)
    take([swap(*send) for send in sends])
    if blocked:
        for halving in (units_0, units_1, heads_0, heads_1):
            while halving.orders[0]:
                halving.take([swap(*send) for send in halving.sends()])
        heads_0, heads_1 = heads_0.result(), heads_1.result()
        total_units = jnp.concatenate([part.result().reshape(3, -1, cut) for part in (units_0, units_1)], 1)
    else:
        def summed(near, far):
            return lax.psum_scatter(jnp.concatenate([near[0], far[0]], -1), "dp", scatter_dimension=1, tiled=True)

        heads_0, heads_1 = summed(*opened[:2]), summed(*closed[:2])
        total_units = [summed(*pair).reshape(3, -1, cut) for pair in ((near_0, far_0), (near_1, far_1))]
        total_units = jnp.concatenate(total_units, 1).astype(f32)

    cols = attention_w.shape[-1]
    lines = 4 * cols
    count = width // (dp * depth)

    def slot_of(s):
        head = (heads_0, heads_1)[s // 2][s % 2 * lines : (s % 2 + 1) * lines]
        share = lax.dynamic_slice_in_dim(heads_1[2 * lines :], (own ^ s) * count, count, 1)
        share = jnp.pad(share, ((0, 0), (0, head.shape[1] - count)))
        return jnp.concatenate([head, share], 0)

    total = slot_of(0).astype(f32)
    for s in range(1, depth):
        total = total + swap(slot_of(s).astype(b16), s).astype(f32)
    small_grad = total[lines : lines + 2 + experts, :count]
    total = total[:lines].reshape(4, cols, -1)
    input_grad = input_gradient(dh, dao, chunk_of(own), sent, inputs, gains)
    output = h + closed_0[0][0].astype(f32) + y1.astype(f32) + y2.astype(f32)

    wg_grad, wu_grad, wd_grad = (total_units[n].reshape(experts, own_units, cut) for n in range(3))
    return (
        output.astype(b16),
        input_grad,
        small_grad[0],
        small_grad[1],
        small_grad[2:].T,
        total[0].T,
        total[1].T,
        total[2].T,
        total[3],
        wg_grad.transpose(0, 2, 1),
        wu_grad.transpose(0, 2, 1),
        wd_grad,
    )


def solution(mesh):
    tokens = P(("dp", "tensor"), None)
    vector = P(("dp", "tensor"))
    return jax.shard_map(
        on_device,
        mesh=mesh,
        in_specs=(tokens, tokens, vector, vector, tokens)
        + (P("dp", "tensor"),) * 3
        + (P("tensor", "dp"), P(None, "dp", "tensor"), P(None, "dp", "tensor"), P(None, "tensor", "dp"))
        + (P("dp", None), P("dp", None)),
        out_specs=(tokens, tokens, vector, vector, tokens)
        + (P("dp", "tensor"),) * 3
        + (P("tensor", "dp"), P(None, "dp", "tensor"), P(None, "dp", "tensor"), P(None, "tensor", "dp")),
        check_vma=False,
    )
```

```python
import jax
import jax.numpy as jnp
from jax import lax
from jax.experimental import pallas as pl
from jax.experimental.pallas import tpu as pltpu
from jax.sharding import PartitionSpec as P

HEAD_DIM = 64
PROMPT = 1024
CONT = 128
CAPACITY = 960
EPS = 1e-06
PAIR = 2 * HEAD_DIM
MIB = 2**20

f32 = jnp.float32
b16 = jnp.bfloat16
NN = (((1,), (0,)), ((), ()))
NT = (((1,), (1,)), ((), ()))
TN = (((0,), (0,)), ((), ()))
INV_SQRT2 = 0.7071067811865476
INV_SQRT_2PI = 0.3989422804014327
MASKED = -1e30
SMALL_ROWS = 32
UNIT_CHUNK = 256
ESTIMATE = 4
FIRST_CHUNKS = 6


def dot(left, right, dims):
    return lax.dot_general(left, right, dims, preferred_element_type=f32)


def params(mib):
    return pltpu.CompilerParams(vmem_limit_bytes=mib * MIB)


def whole(*_):
    return (0, 0)


def unit_of(values):
    scale = lax.rsqrt(jnp.mean(values * values, -1, keepdims=True) + EPS)
    return values * scale, scale


def normal(v):
    bell = jnp.exp(-0.5 * v * v)
    t = 1.0 / (1.0 + (0.3275911 * INV_SQRT2) * jnp.abs(v))
    poly = t * (0.127414796 + t * (-0.142248368 + t * (0.710706871 + t * (-0.726576014 + t * 0.530702715))))
    tail = poly * bell
    return jnp.where(v < 0.0, tail, 1.0 - tail), INV_SQRT_2PI * bell


def keep_mask(ids, order, experts):
    rows = ids.shape[1]
    pairs = ids.shape[0] * rows
    bits = pairs.bit_length()

    def body(ids_ref, order_ref, keep_ref):
        ids_v = ids_ref[...]
        order_v = order_ref[...]
        sub = lax.broadcasted_iota(jnp.int32, (128, rows), 0)
        out = jnp.zeros((128, rows), f32)
        for expert in range(experts):
            mine = ids_v == expert
            bound = jnp.zeros((1, 1), jnp.int32)
            for bit in range(bits - 1, -1, -1):
                trial = bound + (1 << bit)
                inside = jnp.where(mine & (order_v < trial), 1.0, 0.0)
                count = jnp.sum(jnp.sum(inside, 1, keepdims=True), 0, keepdims=True)
                bound = jnp.where(count <= CAPACITY, trial, bound)
            kept = jnp.sum(jnp.where(mine & (order_v < bound), 1.0, 0.0), 0, keepdims=True)
            out = jnp.where((sub < 2 * experts) & (sub % experts == expert), kept, out)
        keep_ref[...] = jnp.transpose(out)

    return pl.pallas_call(
        body,
        out_shape=jax.ShapeDtypeStruct((rows, 128), f32),
        compiler_params=params(32),
    )(ids, order)


def attention_forward(at, slots, gains, weights):
    rows, width = slots[0].shape
    groups, _, _, cols = weights.shape
    tall = PROMPT + rows
    subs = rows // CONT
    pairs = cols // PAIR
    keys = PROMPT + CONT

    def body(at_ref, x0, x1, x2, x3, gain_ref, w_ref, a_out, q_ref, k_ref, v_ref, p_ref, inv_ref, c_ref, h_ref, b_ref, xs, acc, a_s, a_sem):
        step = pl.program_id(0)
        t = at_ref[0]
        a_ref = a_s
        store = pltpu.make_async_copy(a_s, a_out, a_sem)

        @pl.when(step == 0)
        def _():
            for s, x in enumerate((x0, x1, x2, x3)):
                xs[s * rows : (s + 1) * rows] = x[...]
            gain = gain_ref[0:1]
            for start in range(0, PROMPT, rows):
                take = min(rows, PROMPT - start)
                slot = jnp.maximum(t - start // rows, 0)
                x = xs[pl.ds(pl.multiple_of(slot * rows, 128), take)].astype(f32)
                a_ref[start : start + take] = (unit_of(x)[0] * gain).astype(b16)
            x = x0[...].astype(f32)
            a_ref[PROMPT:tall] = (unit_of(x)[0] * gain).astype(b16)
            acc[...] = x
            store.start()

        q = dot(a_ref[PROMPT:tall], w_ref[0, 0], NN).astype(b16) * jnp.asarray(0.125, b16)
        kv = dot(a_ref[...], jnp.concatenate([w_ref[0, 1], w_ref[0, 2]], 1), NN).astype(b16)
        k, v = kv[:, :cols], kv[:, cols:]
        q_ref[...] = q
        k_ref[...] = k
        v_ref[...] = v
        low = lax.broadcasted_iota(jnp.int32, (CONT, PAIR), 1) < HEAD_DIM
        row = lax.broadcasted_iota(jnp.int32, (2 * CONT, PROMPT), 0) % CONT
        past = lax.broadcasted_iota(jnp.int32, (2 * CONT, PROMPT), 1) - row
        own_ok = lax.broadcasted_iota(jnp.int32, (2 * CONT, CONT), 1) <= (
            lax.broadcasted_iota(jnp.int32, (2 * CONT, CONT), 0) % CONT
        )
        lane = lax.broadcasted_iota(jnp.int32, (2 * CONT, 128), 1)
        inverses = jnp.zeros((2 * CONT, 128), f32)
        zero = jnp.zeros((), b16)
        for pair in range(pairs):
            lanes = slice(pair * PAIR, (pair + 1) * PAIR)
            kp, vp = k[:PROMPT, lanes], v[:PROMPT, lanes]
            for sub in range(subs):
                unit = pair * subs + sub
                own = slice(PROMPT + sub * CONT, PROMPT + (sub + 1) * CONT)
                q2 = q[sub * CONT : (sub + 1) * CONT, lanes]
                qs = jnp.concatenate([jnp.where(low, q2, zero), jnp.where(low, zero, q2)], 0)
                first = t * rows + sub * CONT
                s1 = jnp.where(past <= first, dot(qs, kp, NT), MASKED)
                s2 = jnp.where(own_ok & (first >= PROMPT), dot(qs, k[own, lanes], NT), MASKED)
                top = jnp.maximum(jnp.max(s1, -1, keepdims=True), jnp.max(s2, -1, keepdims=True))
                e1 = jnp.exp(s1 - top)
                e2 = jnp.exp(s2 - top)
                inv = 1.0 / (jnp.sum(e1, -1, keepdims=True) + jnp.sum(e2, -1, keepdims=True))
                inverses = jnp.where(lane == unit, inv, inverses)
                p1 = e1.astype(b16)
                p2 = e2.astype(b16)
                at_p = slice(unit * 2 * CONT, (unit + 1) * 2 * CONT)
                p_ref[0, at_p, :PROMPT] = p1
                p_ref[0, at_p, PROMPT:] = p2
                c2 = (dot(p1, vp, NN) + dot(p2, v[own, lanes], NN)) * inv
                c_ref[sub * CONT : (sub + 1) * CONT, lanes] = jnp.where(low, c2[:CONT], c2[CONT:]).astype(b16)
        inv_ref[0] = inverses
        acc[...] += dot(c_ref[...], w_ref[0, 3], NT)

        @pl.when(step == groups - 1)
        def _():
            store.wait()
            h = acc[...]
            h_ref[...] = h
            b_ref[...] = (unit_of(h)[0] * gain_ref[1:2]).astype(b16)

    def by_group(i, at):
        return (0, i)

    return pl.pallas_call(
        body,
        grid_spec=pltpu.PrefetchScalarGridSpec(
            num_scalar_prefetch=1,
            grid=(groups,),
            in_specs=[pl.BlockSpec((rows, width), whole)] * 4
            + [
                pl.BlockSpec(gains.shape, whole),
                pl.BlockSpec((1, 4, width, cols), lambda i, at: (i, 0, 0, 0)),
            ],
            out_specs=[
                pl.BlockSpec(memory_space=pl.ANY),
                pl.BlockSpec((rows, cols), by_group),
                pl.BlockSpec((tall, cols), by_group),
                pl.BlockSpec((tall, cols), by_group),
                pl.BlockSpec((1, 2 * pairs * rows, keys), lambda i, at: (i, 0, 0)),
                pl.BlockSpec((1, 2 * CONT, 128), lambda i, at: (i, 0, 0)),
                pl.BlockSpec((rows, cols), by_group),
                pl.BlockSpec((rows, width), whole),
                pl.BlockSpec((rows, width), whole),
            ],
            scratch_shapes=[
                pltpu.VMEM((4 * rows, width), b16),
                pltpu.VMEM((rows, width), f32),
                pltpu.VMEM((tall, width), b16),
                pltpu.SemaphoreType.DMA,
            ],
        ),
        out_shape=[
            jax.ShapeDtypeStruct((tall, width), b16),
            jax.ShapeDtypeStruct((rows, width), b16),
            jax.ShapeDtypeStruct((tall, width), b16),
            jax.ShapeDtypeStruct((tall, width), b16),
            jax.ShapeDtypeStruct((groups, 2 * pairs * rows, keys), b16),
            jax.ShapeDtypeStruct((groups, 2 * CONT, 128), f32),
            jax.ShapeDtypeStruct((rows, width), b16),
            jax.ShapeDtypeStruct((rows, width), f32),
            jax.ShapeDtypeStruct((rows, width), b16),
        ],
        compiler_params=params(56),
        cost_estimate=pl.CostEstimate(
            flops=(2 * width * width * (2 * tall + 2 * rows) + 8 * rows * keys * width) // ESTIMATE,
            bytes_accessed=60 * MIB // ESTIMATE,
            transcendentals=rows * keys * 16,
        ),
    )(at, *slots, gains, weights)


def attention_backward(me, base, count, given, rest, gains, a, q, k, v, p, inv, c, weights, parts):
    opens = base == 0
    rows, width = q.shape
    _, _, _, cols = weights.shape
    tall = PROMPT + rows
    padded = -(-PROMPT // rows) * rows
    subs = rows // CONT
    pairs = cols // PAIR
    keys = PROMPT + CONT
    cut = width // parts
    blocked = cut % 128 == 0
    places, lanes_out = (parts // 2, cut) if blocked else (1, width // 2)

    def body(me_ref, *refs):
        n_given = 6 if opens else 2
        given_refs = refs[:n_given]
        gain_ref, a_ref, q_ref, k_ref, v_ref, p_ref, inv_ref, c_ref, w_ref = refs[n_given : n_given + 9]
        rest_refs = refs[n_given + 9 : n_given + 9 + len(rest)]
        refs = refs[n_given + 9 + len(rest) :]
        near, far, first_out, row_out, *refs = refs
        if opens:
            sum_ref, *refs = refs
        do, ds, dqs, held, *more = refs
        step = pl.program_id(0)
        acc = more[0]

        @pl.when(step == 0)
        def _():
            if opens:
                h_ref, dy_ref, *part_refs = given_refs
                d0, d1 = (r[...].astype(f32) for r in part_refs[:2])
                dn = d0 + d1 + jnp.concatenate([r[...] for r in part_refs[2:]], 0).astype(f32)
                gain = gain_ref[1:2]
                unit, scale = unit_of(h_ref[...])
                along = dn * gain
                inner = jnp.mean(along * unit, -1, keepdims=True)
                dh = dy_ref[...].astype(f32) + scale * (along - unit * inner)
                row_out[...] = dh
                do[...] = dh.astype(b16)
                sum_ref[...] = jnp.broadcast_to(jnp.sum(dn * unit, 0, keepdims=True), sum_ref.shape)
                acc[...] = jnp.zeros_like(acc)
            else:
                do[...] = given_refs[0][...].astype(b16)
                acc[...] = given_refs[1][...].astype(f32)

        low = lax.broadcasted_iota(jnp.int32, (CONT, PAIR), 1) < HEAD_DIM
        zero = jnp.zeros((), b16)

        def stacked(two):
            return jnp.concatenate([jnp.where(low, two, zero), jnp.where(low, zero, two)], 0)

        def cut_out(start_line, piece):
            count = piece.shape[0]
            span = pl.ds(start_line, count)
            held[:count] = piece
            for s in range(parts if blocked else 2):
                start = (me_ref[0] ^ s) * cut if blocked else s * lanes_out
                lanes = pl.ds(pl.multiple_of(start, lanes_out), lanes_out)
                (far if s % 2 else near)[s // 2, span] = held[:count, lanes]

        def weight_out(kind, left, right, dims):
            value = dot(left, right, dims).astype(b16)
            for n in range(value.shape[0] // cols):
                piece = value[n * cols : (n + 1) * cols]
                line = (kind + n) * cols
                cut_out(line if opens else pl.multiple_of(step * 4 * cols + line, 128), piece)

        dc = dot(do[...], w_ref[0, 3], NN).astype(b16)
        weight_out(3, c_ref[...], do[...], TN)
        dks, dvs = [], []
        for pair in range(pairs):
            lanes = slice(pair * PAIR, (pair + 1) * PAIR)
            kp, vp = k_ref[:PROMPT, lanes], v_ref[:PROMPT, lanes]
            qall, dcall, dko, dvo = [], [], [], []
            for sub in range(subs):
                n = pair * subs + sub
                own = slice(PROMPT + sub * CONT, PROMPT + (sub + 1) * CONT)
                mine = slice(sub * CONT, (sub + 1) * CONT)
                at_p = slice(n * 2 * CONT, (n + 1) * 2 * CONT)
                dcs = (stacked(dc[mine, lanes]).astype(f32) * inv_ref[0][:, n : n + 1]).astype(b16)
                qs = stacked(q_ref[mine, lanes])
                cs = stacked(c_ref[mine, lanes])
                delta = jnp.sum(dcs.astype(f32) * cs.astype(f32), -1, keepdims=True)
                p1 = p_ref[0, at_p, :PROMPT]
                p2 = p_ref[0, at_p, PROMPT:]
                ds1 = (p1.astype(f32) * (dot(dcs, vp, NT) - delta)).astype(b16)
                ds2 = (p2.astype(f32) * (dot(dcs, v_ref[own, lanes], NT) - delta)).astype(b16)
                ds[sub * 2 * CONT : (sub + 1) * 2 * CONT] = ds1
                dq2 = (dot(ds1, kp, NN) + dot(ds2, k_ref[own, lanes], NN)) * 0.125
                dqs[mine, lanes] = jnp.where(low, dq2[:CONT], dq2[CONT:]).astype(b16)
                dko.append(dot(qs, ds2, TN).astype(b16))
                dvo.append(dot(dcs, p2, TN).astype(b16))
                qall.append(qs)
                dcall.append(dcs)
            span = slice(pair * 2 * rows, (pair + 1) * 2 * rows)
            dkp = dot(jnp.concatenate(qall, 0), ds[...], TN).astype(b16)
            dvp = dot(jnp.concatenate(dcall, 0), p_ref[0, span, :PROMPT], TN).astype(b16)
            dks.append(jnp.concatenate([dkp] + dko, 1))
            dvs.append(jnp.concatenate([dvp] + dvo, 1))
        turned = jnp.concatenate(dks + dvs, 0)
        dq = dqs[...]
        weight_out(0, dq, a_ref[PROMPT:tall], TN)
        weight_out(1, turned, a_ref[...], NN)
        acc[...] += dot(jnp.transpose(turned), jnp.concatenate([w_ref[0, 1], w_ref[0, 2]], 1), NT)
        acc[PROMPT:] += dot(dq, w_ref[0, 0], NT)

        @pl.when(step == count - 1)
        def _():
            if opens:
                first_out[...] = acc[...].astype(b16)
            else:
                first_out[:PROMPT] = acc[:PROMPT].astype(b16)
                if padded > PROMPT:
                    first_out[PROMPT:] = jnp.zeros((padded - PROMPT, width), b16)
                row_out[...] = acc[PROMPT:]
                total = jnp.sum(acc[...] * a_ref[...].astype(f32), 0, keepdims=True)
                sums_ref, router_ref = rest_refs
                rows_out = jnp.concatenate(
                    [total / gain_ref[0:1], sums_ref[0:1], router_ref[...], jnp.zeros((SMALL_ROWS - 10, width), f32)], 0
                )
                cut_out(count * 4 * cols, rows_out.astype(b16))

    def by_group(i, me):
        return (0, base + i)

    row_spec = pl.BlockSpec((rows, width), whole)
    half_spec = pl.BlockSpec((rows // 2, width), whole)
    tall_spec = pl.BlockSpec((tall, width), whole)
    lines = count * 4 * cols + (0 if opens else SMALL_ROWS)
    if opens:
        first_spec, first_shape = tall_spec, jax.ShapeDtypeStruct((tall, width), b16)
    else:
        first_spec, first_shape = pl.BlockSpec((padded, width), whole), jax.ShapeDtypeStruct((padded, width), b16)
    return pl.pallas_call(
        body,
        grid_spec=pltpu.PrefetchScalarGridSpec(
            num_scalar_prefetch=1,
            grid=(count,),
        in_specs=([row_spec] * 4 + [half_spec] * 2 if opens else [row_spec, tall_spec])
        + [
            pl.BlockSpec(gains.shape, whole),
            tall_spec,
            pl.BlockSpec((rows, cols), by_group),
            pl.BlockSpec((tall, cols), by_group),
            pl.BlockSpec((tall, cols), by_group),
            pl.BlockSpec((1, 2 * pairs * rows, keys), lambda i, me: (base + i, 0, 0)),
            pl.BlockSpec((1, 2 * CONT, 128), lambda i, me: (base + i, 0, 0)),
            pl.BlockSpec((rows, cols), by_group),
            pl.BlockSpec((1, 4, width, cols), lambda i, me: (base + i, 0, 0, 0)),
        ]
        + [pl.BlockSpec((8, width), whole)] * len(rest),
        out_specs=[
            pl.BlockSpec((places, 4 * cols, lanes_out), lambda i, me: (0, i, 0))
            if opens
            else pl.BlockSpec((places, lines, lanes_out), lambda i, me: (0, 0, 0))
        ]
        * 2
        + [first_spec, row_spec]
        + ([pl.BlockSpec((8, width), whole)] if opens else []),
        scratch_shapes=[
            pltpu.VMEM((rows, width), b16),
            pltpu.VMEM((2 * rows, PROMPT), b16),
            pltpu.VMEM((rows, cols), b16),
            pltpu.VMEM((cols, width), b16),
        ]
        + [pltpu.VMEM((tall, width), f32)],
        ),
        out_shape=[
            jax.ShapeDtypeStruct((places, lines, lanes_out), b16),
            jax.ShapeDtypeStruct((places, lines, lanes_out), b16),
            first_shape,
            jax.ShapeDtypeStruct((rows, width), f32),
        ]
        + ([jax.ShapeDtypeStruct((8, width), f32)] if opens else []),
        compiler_params=params(60),
        cost_estimate=pl.CostEstimate(
            flops=count * (width * width * (2 * tall + 2 * rows) + 4 * rows * keys * width) // ESTIMATE,
            bytes_accessed=count * 20 * MIB // ESTIMATE,
            transcendentals=0,
        ),
    )(me, *given, gains, a, q, k, v, p, inv, c, weights, *rest)


def experts_blocks(blocks, given, begun, place, keep, router, weights, start, own, experts, ends):
    width, one = router.shape[0], given[0].shape[0] // (2 if ends else 1)
    units = weights.shape[1]
    n_given, n_begun = len(given), len(begun)
    met = range(start // own, (start + units - 1) // own + 1)

    def body(blocks_ref, *refs):
        given_refs = refs[:n_given]
        keep_ref, r_ref, wg_ref, wu_ref, wd_ref = refs[n_given + n_begun : n_given + n_begun + 5]
        refs = refs[n_given + n_begun + 5 :]
        b_v, dy_v, keep = given_refs[0][...], given_refs[1][...], keep_ref[...]
        if ends:
            y_ref, db_ref, rg_ref, z_ref, dg_ref, du_ref = refs
        else:
            b_ref, dy_ref, y_ref, db_ref, dgates_ref, z_ref, dg_ref, du_ref = refs
            b_ref[...] = b_v
            dy_ref[...] = dy_v
        lane = lax.broadcasted_iota(jnp.int32, (one, 128), 1)
        col = lax.broadcasted_iota(jnp.int32, (one, units), 1)
        logits = dot(b_v, r_ref[...], NN)
        live = lane < experts
        top = jnp.max(jnp.where(live, logits, MASKED), -1, keepdims=True)
        grown = jnp.exp(jnp.where(lane < 2 * experts, logits, MASKED) - top)
        share = grown / jnp.sum(jnp.where(live, grown, 0.0), -1, keepdims=True)
        gates = share.astype(b16).astype(f32) * keep

        g = dot(b_v, wg_ref[0], NT)
        u = dot(b_v, wu_ref[0], NT)
        dz_plain = dot(dy_v, wd_ref[0], NT)
        gate = gates[:, met[-1] : met[-1] + 1]
        for expert in met[-2::-1]:
            gate = jnp.where(col < (expert + 1) * own - start, gates[:, expert : expert + 1], gate)
        cdf, pdf = normal(g)
        act = g * cdf
        z = (act * u).astype(b16).astype(f32)
        along = dz_plain * z
        dgates = given_refs[4][...] if ends else jnp.zeros((one, 128), f32)
        for expert in met:
            low, high = max(expert * own - start, 0), min((expert + 1) * own - start, units)
            inner_low, inner_high = -(-low // 128) * 128, high // 128 * 128
            part = jnp.sum(along[:, inner_low:inner_high], -1, keepdims=True)
            if low < inner_low:
                edge = along[:, inner_low - 128 : inner_low]
                part += jnp.sum(jnp.where(lane >= low % 128, edge, 0.0), -1, keepdims=True)
            if inner_high < high:
                edge = along[:, inner_high : inner_high + 128]
                part += jnp.sum(jnp.where(lane < high % 128, edge, 0.0), -1, keepdims=True)
            dgates += jnp.where(lane % experts == expert, part, 0.0)
        dz = dz_plain * gate
        dg = (dz * u * (cdf + g * pdf)).astype(b16)
        du = (dz * act).astype(b16)
        zg = (z * gate).astype(b16)
        z_ref[...] = zg
        dg_ref[...] = dg
        du_ref[...] = du
        y = dot(zg, wd_ref[0], NN)
        db = dot(dg, wg_ref[0], NN) + dot(du, wu_ref[0], NN)
        if not ends:
            y_ref[...] = y
            db_ref[...] = db
            dgates_ref[...] = dgates
        else:
            dprob = dgates * keep
            inner = jnp.sum(jnp.where(lane < experts, share * dprob, 0.0), -1, keepdims=True)
            dl = jnp.where(lane < 2 * experts, share * (dprob - inner), 0.0)
            head = dl.astype(b16).astype(f32)
            split = jnp.where(lane < experts, head, dl - head).astype(b16)
            rg_ref[0] = dot(split, b_v, TN)[:8]
            y_ref[0] = (y + given_refs[2][...]).astype(b16)
            db_ref[0] = (db + given_refs[3][...] + dot(split, r_ref[...], NT)).astype(b16)

    def weight(kind):
        return pl.BlockSpec((1, units, width), lambda i, at: (kind, 0, 0))

    def by_place(i, at):
        return (i if ends else place, 0)

    wide = pl.BlockSpec((one, width), by_place)
    thin = pl.BlockSpec((one, 128), by_place)
    hidden = pl.BlockSpec((one, units), by_place)
    hidden_shape = jax.ShapeDtypeStruct((2 * one, units), b16)
    if ends:
        own_block = pl.BlockSpec((1, one, width), lambda i, at: (i, 0, 0))
        outs = [(own_block, jax.ShapeDtypeStruct((2, one, width), b16))] * 2
        outs += [(pl.BlockSpec((1, 8, width), lambda i, at: (i, 0, 0)), jax.ShapeDtypeStruct((2, 8, width), f32))]
    else:
        outs = [(wide, jax.ShapeDtypeStruct((2 * one, width), b16))] * 2
        outs += [(wide, jax.ShapeDtypeStruct((2 * one, width), f32))] * 2
        outs += [(thin, jax.ShapeDtypeStruct((2 * one, 128), f32))]
    outs += [(hidden, hidden_shape)] * 3
    return pl.pallas_call(
        body,
        grid_spec=pltpu.PrefetchScalarGridSpec(
            num_scalar_prefetch=1,
            grid=(2 if ends else 1,),
            in_specs=([wide] * 4 + [thin] if ends else [pl.BlockSpec((one, width), whole)] * 2)
            + [pl.BlockSpec(memory_space=pl.ANY)] * n_begun
            + [
                pl.BlockSpec((one, 128), lambda i, at: (at[i], 0)),
                pl.BlockSpec((width, 128), whole),
                weight(0),
                weight(1),
                weight(2),
            ],
            out_specs=[spec for spec, _ in outs],
        ),
        out_shape=[shape for _, shape in outs],
        input_output_aliases={1 + n_given + n: n for n in range(n_begun)},
        compiler_params=params(60),
        cost_estimate=pl.CostEstimate(
            flops=(24 if ends else 12) * one * width * units // ESTIMATE,
            bytes_accessed=(6 * units * width + 6 * one * units) // ESTIMATE,
            transcendentals=2 * one * units,
        ),
    )(blocks, *given, *begun, keep, router, weights, weights, weights)


def experts_weights(me, bs, dys, zs, dgs, dus, parts):
    pieces = len(bs)
    rows, width = bs[0].shape
    units = zs[0].shape[1]
    chunk = UNIT_CHUNK
    cut = width // parts
    blocked = cut % 128 == 0

    def body(me_ref, *refs):
        b_refs, dy_refs, z, dg, du = (refs[n * pieces : (n + 1) * pieces] for n in range(5))
        near, far, held = refs[5 * pieces :]
        for kind, (left, right) in enumerate(((dg, b_refs), (du, b_refs), (z, dy_refs))):
            value = dot(left[0][...], right[0][...], TN)
            for n in range(1, pieces):
                value += dot(left[n][...], right[n][...], TN)
            held[kind] = value.astype(b16)
            for s in range(parts if blocked else 0):
                lanes = pl.ds(pl.multiple_of((me_ref[0] ^ s) * cut, cut), cut)
                (far if s % 2 else near)[s // 2, kind] = held[kind, :, lanes]
            if not blocked:
                near[0, kind] = held[kind, :, : width // 2]
                far[0, kind] = held[kind, :, width // 2 :]

    places, lanes = (parts // 2, cut) if blocked else (1, width // 2)
    return pl.pallas_call(
        body,
        grid_spec=pltpu.PrefetchScalarGridSpec(
            num_scalar_prefetch=1,
            grid=(units // chunk,),
            in_specs=[pl.BlockSpec((rows, width), whole)] * (2 * pieces)
            + [pl.BlockSpec((rows, chunk), lambda i, me: (0, i))] * (3 * pieces),
            out_specs=[pl.BlockSpec((places, 3, chunk, lanes), lambda i, me: (0, 0, i, 0))] * 2,
            scratch_shapes=[pltpu.VMEM((3, chunk, width), b16)],
        ),
        out_shape=[jax.ShapeDtypeStruct((places, 3, units, lanes), b16)] * 2,
        compiler_params=params(56),
        cost_estimate=pl.CostEstimate(
            flops=(6 * pieces * rows * width * units) // ESTIMATE,
            bytes_accessed=(6 * units * width + 6 * pieces * rows * units) // ESTIMATE,
            transcendentals=0,
        ),
    )(me, *bs, *dys, *zs, *dgs, *dus)


class Halving:
    def __init__(self, near, other, low, high):
        places = near.shape[0]
        half = (high - low) // 2
        bits = [1 << n for n in range(places.bit_length() - 1)]
        self.orders = [bits, bits[::-1]]
        self.held = []
        for path in range(2):
            span = slice(low + path * half, low + (path + 1) * half)
            self.held.append({s: near[s, span].astype(f32) + other[s, span].astype(f32) for s in range(places)})

    def sends(self):
        self.bits = [order.pop(0) for order in self.orders]
        out = []
        for held, bit in zip(self.held, self.bits):
            out.append((jnp.concatenate([held[s] for s in held if s & bit], 0).astype(b16), 2 * bit, "dp"))
        return out

    def take(self, got):
        for path, (held, bit, came) in enumerate(zip(self.held, self.bits, got)):
            away = [s for s in held if s & bit]
            size = came.shape[0] // len(away)
            self.held[path] = {s ^ bit: held[s ^ bit] + came[n * size : (n + 1) * size].astype(f32) for n, s in enumerate(away)}

    def result(self):
        return jnp.concatenate([held[0] for held in self.held], 0)


def input_gradient(dh, own, piece, sent, x, gains):
    rows, width = dh.shape

    def body(dh_ref, own_ref, piece_ref, sent_ref, x_ref, gain_ref, out_ref):
        da = own_ref[...] + (piece_ref[...].astype(f32) + sent_ref[...].astype(f32))
        unit, scale = unit_of(x_ref[...].astype(f32))
        along = da * gain_ref[0:1]
        inner = jnp.mean(along * unit, -1, keepdims=True)
        out_ref[...] = dh_ref[...] + scale * (along - unit * inner)

    block = pl.BlockSpec((CONT, width), lambda i: (i, 0))
    return pl.pallas_call(
        body,
        grid=(rows // CONT,),
        in_specs=[block] * 5 + [pl.BlockSpec(gains.shape, whole)],
        out_specs=block,
        out_shape=jax.ShapeDtypeStruct((rows, width), f32),
        compiler_params=params(32),
    )(dh, own, piece, sent, x, gains)


def on_device(inputs, cotangent, attn_gain, moe_gain, router, w_query, w_key, w_value, w_out, w_gate, w_up, w_down, expert_ids, priority):
    rows, width = inputs.shape
    experts, cut, own_units = w_gate.shape
    units = experts * own_units
    dp = lax.axis_size("dp")
    depth = lax.axis_size("tensor")
    own = lax.axis_index("tensor")
    me = lax.axis_index("dp")
    at = jnp.full((1,), own, jnp.int32)
    here = jnp.full((1,), me, jnp.int32)
    up = [(i, i + 1) for i in range(depth - 1)]
    down = [(i + 1, i) for i in range(depth - 1)]
    together = lax.optimization_barrier

    def swap(value, bits, axis="tensor"):
        size = depth if axis == "tensor" else dp
        return lax.ppermute(value, axis, [(i, i ^ bits) for i in range(size)])

    def raised(value):
        return lax.ppermute(value, "tensor", up)

    mine = jnp.stack([w_query, w_key, w_value, w_out.T])
    far = swap(mine, 2)
    attention_w = jnp.stack([mine, swap(mine, 1), far, swap(far, 1)])
    attention_w = lax.all_gather(attention_w, "dp", axis=2, tiled=True)

    small = jnp.concatenate([attn_gain[None], moe_gain[None], router.T, jnp.zeros((2, router.shape[0]), b16)], 0)

    def doubled(small, other, index, bit):
        return jnp.where(index & bit != 0, jnp.concatenate([other, small], 1), jnp.concatenate([small, other], 1))

    for bit in [1 << n for n in range(dp.bit_length() - 1)]:
        small = doubled(small, swap(small, bit, "dp"), me, bit)
    x1, other = together((raised(inputs), swap(small, 1)))
    small = doubled(small, other, own, 1)
    x2, other = together((raised(x1), swap(small, 2)))
    small = doubled(small, other, own, 2)
    small = small.reshape(8, depth, dp, -1).swapaxes(1, 2).reshape(8, width)
    x3 = raised(x2)
    gains = small.astype(f32)
    router_full = small[2 : 2 + experts].T
    router_wide = jnp.concatenate(
        [router_full, router_full, jnp.zeros((width, 128 - 2 * experts), b16)], 1
    )
    keep = keep_mask(expert_ids.T, priority.reshape(-1, 2).T, experts)

    shards = [w_gate.transpose(0, 2, 1), w_up.transpose(0, 2, 1), w_down]
    shards = jnp.stack([shard.reshape(units, cut) for shard in shards])
    middle = FIRST_CHUNKS * UNIT_CHUNK
    halves = [
        lax.all_gather(piece, "dp", axis=2, tiled=True)
        for piece in (shards[:, :middle], shards[:, middle:])
    ]

    x3, gains, dy0, keep, router_wide = together((x3, gains, cotangent, keep, router_wide))
    dy1, dy2 = swap(dy0, 1), swap(dy0, 2)
    a, q, k, v, p, inv, c, h, b = attention_forward(at, (inputs, x1, x2, x3), gains, attention_w)
    b, dy1, dy2 = together((b, dy1, dy2))
    b1, b2 = swap(b, 1), swap(b, 2)
    bs, dys = [b], [dy0]

    def open_block(slot, begun):
        block = jnp.full((1,), own ^ slot, jnp.int32)
        return experts_blocks(block, (bs[slot], dys[slot]), begun, slot % 2, keep, router_wide, halves[0], 0, own_units, experts, False)

    def close_pair(pair, given):
        blocks = jnp.stack([own ^ (2 * pair), own ^ (2 * pair + 1)]).astype(jnp.int32)
        return experts_blocks(blocks, given, (), 0, keep, router_wide, halves[1], middle, own_units, experts, True)

    opened_0 = open_block(0, ())
    opened_0, b2 = together((opened_0, b2))
    bs += [b1, b2, swap(b2, 1)]
    dys += [dy1, dy2, swap(dy2, 1)]
    opened_0 = open_block(1, opened_0)
    opened_1 = open_block(3, open_block(2, ()))
    opened_0, opened_1 = together((opened_0, opened_1))
    closed_1 = close_pair(1, opened_1[:5])
    opened_0, closed_1 = together((opened_0, closed_1))
    near3 = swap(closed_1[1][1], 1)
    closed_0 = close_pair(0, opened_0[:5])
    closed_0, near3 = together((closed_0, near3))
    joined = [opened_0[0], opened_1[0]], [opened_0[1], opened_1[1]]
    blocked = cut % 128 == 0

    def stage(sends, given=(), work=None):
        values = tuple(value for value, *_ in sends)
        if work is None:
            values = together(values)
        else:
            values, given = together((values, given))
        got = tuple(swap(value, *how) for value, (_, *how) in zip(values, sends))
        return together((got, given if work is None else work(given)))

    def joint(*halvings):
        lists = {}
        for halving in halvings:
            if halving is not None and halving.orders[0]:
                for path, (value, *how) in enumerate(halving.sends()):
                    lists.setdefault(tuple(how), []).append((halving, path, value))
        sends = [(jnp.concatenate([value for *_, value in items], 0), *how) for how, items in lists.items()]

        def take(got):
            came = {}
            for whole_value, items in zip(got, lists.values()):
                start = 0
                for halving, path, value in items:
                    came.setdefault(id(halving), (halving, {}))[1][path] = whole_value[start : start + value.shape[0]]
                    start += value.shape[0]
            for halving, paths in came.values():
                halving.take([paths[0], paths[1]])

        return sends, take

    def flat(value):
        return value.reshape(value.shape[0], -1, value.shape[-1])

    def weights_of(units):
        hidden = (opened_0[5:], opened_1[5:]) if units == 0 else (closed_0[3:], closed_1[3:])
        return lambda given: [flat(v) for v in experts_weights(here, *given, *zip(*hidden), dp)]

    def core_send(far):
        return [(far, 1, "dp")] if blocked else []

    def halving_of(near, got):
        return Halving(near, got[0], 0, near.shape[1]) if blocked else None

    d2 = closed_1[1][0] + near3
    half = rows // 2
    got, (near_0, far_0) = stage([(d2[:half], 2), (closed_1[0][1], 1)], joined, weights_of(0))
    d2_low, near3 = got
    y2 = closed_1[0][0] + near3
    sends = core_send(far_0)
    got, (near_1, far_1) = stage([(closed_0[1][1], 1), (d2[half:], 2)] + sends, joined, weights_of(1))
    d1, d2_high = got[:2]
    units_0 = halving_of(near_0, got[2:])

    rg = (closed_0[2] + closed_1[2]).sum(0)
    rg = jnp.concatenate([rg[:experts] + rg[experts : 2 * experts], jnp.zeros((8 - experts, width), f32)], 0)

    def backward(base, rest):
        return lambda given: attention_backward(here, base, 2, given, rest, gains, a, q, k, v, p, inv, c, attention_w, dp)

    given = (h, cotangent, closed_0[1][0], d1, d2_low, d2_high)
    sends, take = joint(units_0)
    got, opened = stage([(closed_0[0][1], 1)] + core_send(far_1) + sends, given, backward(0, ()))
    y1 = got[0]
    units_1 = halving_of(near_1, got[1:])
    take(got[2:])
    sends, take = joint(units_1, units_0)
    got, closed = stage([(y2, 2)] + core_send(opened[1]) + sends, (opened[3], opened[2]), backward(2, (opened[4], rg)))
    y2 = got[0]
    heads_0 = halving_of(opened[0], got[1:])
    take(got[2:])
    dap, dao, dh = closed[2], closed[3], opened[3]

    def chunk_of(index):
        start = jnp.clip(index, 0, dap.shape[0] // rows - 1) * rows
        piece = lax.dynamic_slice_in_dim(dap, start, rows, 0)
        valid = (index >= 0) & (index < dap.shape[0] // rows)
        return jnp.where(valid, piece, jnp.zeros((), b16))

    def hop(index, sent=None):
        piece = chunk_of(own - depth + index)
        return lax.ppermute(piece if sent is None else piece + sent, "tensor", down)

    sent = hop(1)
    sends, take = joint(units_1, heads_0)
    got, sent = stage(core_send(closed[1]) + sends, sent)
    heads_1 = halving_of(closed[0], got)
    take(got[1:])
    sent = hop(2, sent)
    sends, take = joint(heads_1, heads_0)
    take([swap(*send) for send in sends])
    sent = hop(3, sent)
    sends, take = joint(heads_1)
    take([swap(*send) for send in sends])
    if blocked:
        for halving in (units_0, units_1, heads_0, heads_1):
            while halving.orders[0]:
                halving.take([swap(*send) for send in halving.sends()])
        heads_0, heads_1 = heads_0.result(), heads_1.result()
        total_units = jnp.concatenate([part.result().reshape(3, -1, cut) for part in (units_0, units_1)], 1)
    else:
        def summed(near, far):
            return lax.psum_scatter(jnp.concatenate([near[0], far[0]], -1), "dp", scatter_dimension=1, tiled=True)

        heads_0, heads_1 = summed(*opened[:2]), summed(*closed[:2])
        total_units = [summed(*pair).reshape(3, -1, cut) for pair in ((near_0, far_0), (near_1, far_1))]
        total_units = jnp.concatenate(total_units, 1).astype(f32)

    cols = attention_w.shape[-1]
    lines = 4 * cols
    count = width // (dp * depth)

    def slot_of(s):
        head = (heads_0, heads_1)[s // 2][s % 2 * lines : (s % 2 + 1) * lines]
        share = lax.dynamic_slice_in_dim(heads_1[2 * lines :], (own ^ s) * count, count, 1)
        share = jnp.pad(share, ((0, 0), (0, head.shape[1] - count)))
        return jnp.concatenate([head, share], 0)

    total = slot_of(0).astype(f32)
    for s in range(1, depth):
        total = total + swap(slot_of(s).astype(b16), s).astype(f32)
    small_grad = total[lines : lines + 2 + experts, :count]
    total = total[:lines].reshape(4, cols, -1)
    input_grad = input_gradient(dh, dao, chunk_of(own), sent, inputs, gains)
    output = h + closed_0[0][0].astype(f32) + y1.astype(f32) + y2.astype(f32)

    wg_grad, wu_grad, wd_grad = (total_units[n].reshape(experts, own_units, cut) for n in range(3))
    return (
        output.astype(b16),
        input_grad,
        small_grad[0],
        small_grad[1],
        small_grad[2:].T,
        total[0].T,
        total[1].T,
        total[2].T,
        total[3],
        wg_grad.transpose(0, 2, 1),
        wu_grad.transpose(0, 2, 1),
        wd_grad,
    )


def solution(mesh):
    tokens = P(("dp", "tensor"), None)
    vector = P(("dp", "tensor"))
    return jax.shard_map(
        on_device,
        mesh=mesh,
        in_specs=(tokens, tokens, vector, vector, tokens)
        + (P("dp", "tensor"),) * 3
        + (P("tensor", "dp"), P(None, "dp", "tensor"), P(None, "dp", "tensor"), P(None, "tensor", "dp"))
        + (P("dp", None), P("dp", None)),
        out_specs=(tokens, tokens, vector, vector, tokens)
        + (P("dp", "tensor"),) * 3
        + (P("tensor", "dp"), P(None, "dp", "tensor"), P(None, "dp", "tensor"), P(None, "tensor", "dp")),
        check_vma=False,
    )
```
